1024 devices in a mesh: replica: 8 (over z), fsdp: 64 (over x_lo, y, core), tensor: 2 (over x_hi).
Axes of the slice: x: 8 (x_hi: 2, x_lo: 4; x = x_hi * 4 + x_lo), y: 8, z: 8, core: 2. Of those that a mesh axis runs over, the one named last changes fastest.
Arguments:
- hidden_in: bfloat16 [65536, 8192], P(('replica', 'fsdp')), may hold values from -500 to 500
- norm_gain: bfloat16 [8192], replicated, may hold values from 0.099609375 to 1.8984375
- key_cotangent: bfloat16 [65536, 512], P(('replica', 'fsdp'), 'tensor'), may hold values from -220 to 220
- inner_params: float32 [8, 8192, 512], P('replica', 'fsdp', 'tensor'), may hold values from -6 to 6
- inner_first: float32 [8, 8192, 512], P('replica', 'fsdp', 'tensor'), may hold values from -6 to 6
- inner_second: float32 [8, 8192, 512], P('replica', 'fsdp', 'tensor'), may hold values from 1 to 10
- frag_local: float32 [8, 8, 8192, 512], P('replica', None, 'fsdp', 'tensor'), may hold values from -6 to 6
- frag_global: float32 [8, 8192, 512], P(None, 'fsdp', 'tensor'), may hold values from -6 to 6
- outer_momentum: float32 [8, 8192, 512], P(None, 'fsdp', 'tensor'), may hold values from -6 to 6
- frag_index: int32 [1], replicated, may hold values from 0 to 7
Outputs:
- new_params: float32 [8, 8192, 512], P('replica', 'fsdp', 'tensor')
- new_first: float32 [8, 8192, 512], P('replica', 'fsdp', 'tensor')
- new_second: float32 [8, 8192, 512], P('replica', 'fsdp', 'tensor')
- new_fragment: float32 [8192, 512], P('fsdp', 'tensor')
- new_momentum: float32 [8192, 512], P('fsdp', 'tensor')
The draws below stay inside these ranges and needn't reach their ends.
All inputs are finite; a program needn't handle non-finite values.
Results may differ from the reference program's by a relative error of at most 0.0029.
Values may be sent and summed in bfloat16 or wider, within the bound.
No kernel may reach another device: no remote copies, remote signals or barrier semaphores. Data moves between devices by JAX's collectives and lax.ppermute only.
A program may use at most 32 MiB of HBM per device.

```python
import math
import jax
import jax.numpy as jnp
from jax import lax

D = 8192
L_FRAG = 8
KC = 512
TOKENS = 8192
ALL_TOKENS = 65536
N_REPLICA = 8


def draw_hidden_in(key, part):
    key = jax.random.fold_in(key, 11)
    keys = jax.random.split(key, 3)
    ramp = jnp.arange(D, dtype=jnp.float32) / max(D - 1, 1)
    feature = jnp.exp(jax.random.uniform(keys[1], (1, D), jnp.float32, 0.0, math.log(10.0)))
    rowscale = jnp.exp(jax.random.uniform(keys[2], (ALL_TOKENS, 1), jnp.float32, 0.0, math.log(4.0)))
    base = jnp.clip(jax.random.normal(keys[0], (ALL_TOKENS, D), jnp.float32), -4.0, 4.0)
    ramp_scale = jnp.sqrt(1.0 + 2.0 * ramp)[None, :]
    return (base * feature * ramp_scale * rowscale).astype(jnp.bfloat16)


def draw_key_cotangent(key, part):
    key = jax.random.fold_in(key, 23)
    keys = jax.random.split(key, 5)
    column = jnp.exp(jax.random.uniform(keys[1], (1, KC), jnp.float32, 0.0, math.log(10.0)))
    rowscale = jnp.exp(jax.random.uniform(keys[2], (ALL_TOKENS, 1), jnp.float32, math.log(0.5), math.log(2.0)))
    order = jax.random.permutation(keys[4], N_REPLICA).astype(jnp.float32)
    level = jnp.exp(math.log(0.2) + math.log(25.0) * (order + 0.5) / N_REPLICA)
    base = jnp.clip(jax.random.normal(keys[0], (ALL_TOKENS, KC), jnp.float32), -4.0, 4.0)
    spread = math.sqrt(29.0 * TOKENS)
    worker = jnp.repeat(8.0 * level / spread, TOKENS, total_repeat_length=ALL_TOKENS)[:, None]
    return (base * column * rowscale * worker).astype(jnp.bfloat16)


def shard_levels(key, shape, shards, smallest, top_value):
    level, own = 1.0, jax.random.fold_in(key, 6)
    for axis_at, shards_of in shards:
        steps = jnp.exp(jax.random.uniform(jax.random.fold_in(own, axis_at), (shards_of,), jnp.float32, smallest / len(shards), top_value / len(shards)))
        level = level * jnp.repeat(steps, shape[axis_at] // shards_of).reshape([-1 if axis == axis_at else 1 for axis in range(len(shape))])
    return level


def scatter_about(stream_key, shape, scale, most, cuts=(), kind=jnp.bfloat16):
    drawn = jax.random.normal(stream_key, shape, jnp.float32) * scale
    if len(cuts) > 0:
        drawn = shard_levels(stream_key, shape, cuts, -0.22, 0.18) * drawn
    return jnp.clip(drawn, min=-most, max=most).astype(kind)


def setup_inputs(seed: int = 0) -> dict:
    key_of = jax.random.split(jax.random.key(seed), 11)
    return {
        "hidden_in": draw_hidden_in(jax.random.fold_in(key_of[10], 71), 0),
        "norm_gain": jnp.clip(1.0 + 0.18 * jax.random.normal(key_of[1], (D,), jnp.float32), 0.099609375, 1.8984375).astype(jnp.bfloat16),
        "key_cotangent": draw_key_cotangent(jax.random.fold_in(key_of[10], 71), 0),
        "inner_params": scatter_about(key_of[3], (N_REPLICA, D, KC), 1.0, 6.0, ((0, 8), (1, 64), (2, 2)), jnp.float32),
        "inner_first": scatter_about(key_of[4], (N_REPLICA, D, KC), 1.0, 6.0, ((0, 8), (1, 64), (2, 2)), jnp.float32),
        "inner_second": jnp.clip(jnp.exp(math.log(10.0) - 2.3025851 * jax.random.uniform(key_of[5], (N_REPLICA, D, KC), jnp.float32) ** shard_levels(key_of[5], (N_REPLICA, D, KC), ((0, 8), (1, 64), (2, 2)), -0.2, 0.2)), 1.0, 10.0),
        "frag_local": scatter_about(key_of[6], (N_REPLICA, L_FRAG, D, KC), 1.0, 6.0, ((0, 8), (2, 64), (3, 2)), jnp.float32),
        "frag_global": scatter_about(key_of[7], (L_FRAG, D, KC), 1.0, 6.0, ((1, 64), (2, 2)), jnp.float32),
        "outer_momentum": scatter_about(key_of[8], (L_FRAG, D, KC), 0.5, 6.0, ((1, 64), (2, 2)), jnp.float32),
        "frag_index": jax.random.randint(key_of[9], (1,), 0, L_FRAG).astype(jnp.int32),
    }


NORM_EPS = 1e-05
CLIP_RMS = 8.0
FIRST_BETA = 0.9
SECOND_BETA = 0.95
FIRST_FIX = 1.0 - 0.9 ** 10
SECOND_FIX = 1.0 - 0.95 ** 10
ADAM_EPS = 1e-08
INNER_RATE = 0.01
DECAY_WEIGHT = 0.1
OUTER_RATE = 0.7
OUTER_BETA = 0.9

def worker_step(packed):
    worker_in, worker_cot, params, first, second, gain_wide = packed
    widened = worker_in.astype(jnp.float32)
    mean_square = lax.optimization_barrier(jnp.mean(widened * widened, axis=1, keepdims=True))
    normed = (widened * lax.rsqrt(mean_square + NORM_EPS) * gain_wide).astype(jnp.bfloat16)
    gradient = jnp.dot(normed.T, worker_cot, preferred_element_type=jnp.float32)
    total_square = jnp.sum(gradient * gradient)
    factor = jnp.minimum(1.0, CLIP_RMS * lax.rsqrt(total_square / (D * KC) + 1e-06))
    clipped = factor * gradient
    new_first = FIRST_BETA * first + (1.0 - FIRST_BETA) * clipped
    new_second = SECOND_BETA * second + (1.0 - SECOND_BETA) * clipped * clipped
    direction = new_first / FIRST_FIX / (jnp.sqrt(new_second / SECOND_FIX) + ADAM_EPS)
    new_params = params - INNER_RATE * (direction + DECAY_WEIGHT * params)
    return (new_params, new_first, new_second)

def reference(hidden_in, norm_gain, key_cotangent, inner_params, inner_first, inner_second, frag_local, frag_global, outer_momentum, frag_index):
    worker_in = hidden_in.reshape(N_REPLICA, TOKENS, D)
    worker_cot = key_cotangent.reshape(N_REPLICA, TOKENS, KC)
    gain_wide = jnp.broadcast_to(norm_gain.astype(jnp.float32)[None, :], (N_REPLICA, D))
    new_params, new_first, new_second = lax.map(worker_step, (worker_in, worker_cot, inner_params, inner_first, inner_second, gain_wide))
    layer_index = frag_index[0].astype(jnp.int32)
    local_layer = lax.dynamic_index_in_dim(frag_local, layer_index, 1, keepdims=False)
    global_layer = lax.dynamic_index_in_dim(frag_global, layer_index, 0, keepdims=False)
    moment_layer = lax.dynamic_index_in_dim(outer_momentum, layer_index, 0, keepdims=False)
    summed = lax.optimization_barrier(jnp.sum(local_layer, axis=0))
    pseudo = global_layer - summed / N_REPLICA
    new_momentum = OUTER_BETA * moment_layer + pseudo
    new_fragment = global_layer - OUTER_RATE * (pseudo + OUTER_BETA * new_momentum)
    return (new_params, new_first, new_second, new_fragment, new_momentum)
```

```python
import jax
import jax.numpy as jnp
from jax import lax
from jax.sharding import Mesh, PartitionSpec as P

NORM_EPS = 1e-05
CLIP_RMS = 8.0
FIRST_BETA = 0.9
SECOND_BETA = 0.95
FIRST_FIX = 1.0 - 0.9**10
SECOND_FIX = 1.0 - 0.95**10
ADAM_EPS = 1e-08
INNER_RATE = 0.01
DECAY_WEIGHT = 0.1
OUTER_RATE = 0.7
OUTER_BETA = 0.9

XL, YN, CORES, XH = 4, 8, 2, 2
CHIP_SCALE = 2.0**-8
X_SCALE = 2.0**-10
Y_SCALE = 2.0**-11


def outer_update(summed, global_layer, moment_layer, workers):
    pseudo = global_layer - summed / workers
    new_momentum = OUTER_BETA * moment_layer + pseudo
    new_fragment = global_layer - OUTER_RATE * (pseudo + OUTER_BETA * new_momentum)
    return (new_fragment, new_momentum)


def swap_x(block, k):
    return lax.ppermute(block, "xl", [(i, i ^ k) for i in range(XL)])


def worker_gradient(hidden_in, norm_gain, key_cotangent):
    x_at, c_at = lax.axis_index("xl"), lax.axis_index("c")
    other_cot = lax.ppermute(key_cotangent, "c", [(0, 1), (1, 0)])
    first_core = c_at == 0
    cot = jnp.concatenate(
        [
            jnp.where(first_core, key_cotangent, other_cot),
            jnp.where(first_core, other_cot, key_cotangent),
        ],
        axis=0,
    )
    widened = hidden_in.astype(jnp.float32)
    mean_square = jnp.mean(widened * widened, axis=1, keepdims=True)
    normed = (
        widened * lax.rsqrt(mean_square + NORM_EPS) * norm_gain.astype(jnp.float32)[None, :]
    ).astype(jnp.bfloat16)
    tokens = hidden_in.shape[0]
    halves = normed.reshape(tokens, XL * YN, CORES, 128).transpose(2, 0, 1, 3)
    halves = lax.all_to_all(halves.reshape(CORES, tokens, XL * YN * 128), "c", 0, 0, tiled=True)
    halves = halves.reshape(CORES * tokens, XL * YN * 128)
    partial = lax.dot_general(
        cot, halves, (((0,), (0,)), ((), ())), preferred_element_type=jnp.float32
    )
    partial = (partial * CHIP_SCALE).astype(jnp.float16)
    blocks = partial.reshape(2, 128, XL, YN, 128)
    x_first = blocks[0].transpose(1, 2, 0, 3)
    y_first = blocks[1].transpose(2, 1, 0, 3)

    y_parts = lax.all_to_all(y_first, "y", 0, 0, tiled=True)
    mine = lax.dynamic_index_in_dim(x_first, x_at, 0, keepdims=False)
    x_sum = mine.astype(jnp.float32)
    for k in range(1, XL):
        part = lax.dynamic_index_in_dim(x_first, x_at ^ k, 0, keepdims=False)
        x_sum = x_sum + swap_x(part, k).astype(jnp.float32)
    x_sum = (x_sum * (X_SCALE / CHIP_SCALE)).astype(jnp.float16)
    y_sum = jnp.sum(y_parts.astype(jnp.float32), axis=0)
    y_sum = (y_sum * (Y_SCALE / CHIP_SCALE)).astype(jnp.float16)

    top = lax.all_to_all(x_sum, "y", 0, 0, tiled=True)
    bottom = lax.dynamic_index_in_dim(y_sum, x_at, 0, keepdims=False).astype(jnp.float32)
    for k in range(1, XL):
        part = lax.dynamic_index_in_dim(y_sum, x_at ^ k, 0, keepdims=False)
        bottom = bottom + swap_x(part, k).astype(jnp.float32)
    top = jnp.sum(top.astype(jnp.float32), axis=0) * (1.0 / X_SCALE)
    return jnp.concatenate([top, bottom * (1.0 / Y_SCALE)], axis=0)


def sum_worker(value):
    devices = XL * YN * CORES * XH
    rows = jnp.broadcast_to(value, (devices, 1, 128))
    rows = lax.all_to_all(rows, ("xl", "y", "c", "xh"), 0, 0, tiled=True)
    return jnp.sum(rows[:, 0, 0])


def on_device(
    hidden_in,
    norm_gain,
    key_cotangent,
    inner_params,
    inner_first,
    inner_second,
    frag_local,
    frag_global,
    outer_momentum,
    frag_index,
):
    layer_index = frag_index[0]
    local_layer = lax.dynamic_index_in_dim(frag_local[0], layer_index, 0, keepdims=False)
    summed = lax.psum(local_layer, "z")

    gradient = worker_gradient(hidden_in, norm_gain, key_cotangent)
    total_square = sum_worker(jnp.sum(gradient * gradient))
    entries = gradient.shape[0] * gradient.shape[1] * XL * YN * CORES * XH
    factor = jnp.minimum(1.0, CLIP_RMS * lax.rsqrt(total_square / entries + 1e-06))
    clipped = factor * gradient.T
    params = inner_params[0]
    new_first = FIRST_BETA * inner_first[0] + (1.0 - FIRST_BETA) * clipped
    new_second = SECOND_BETA * inner_second[0] + (1.0 - SECOND_BETA) * clipped * clipped
    direction = new_first / FIRST_FIX / (jnp.sqrt(new_second / SECOND_FIX) + ADAM_EPS)
    new_params = params - INNER_RATE * (direction + DECAY_WEIGHT * params)

    global_layer = lax.dynamic_index_in_dim(frag_global, layer_index, 0, keepdims=False)
    moment_layer = lax.dynamic_index_in_dim(outer_momentum, layer_index, 0, keepdims=False)
    workers = lax.axis_size("z")
    new_fragment, new_momentum = outer_update(summed, global_layer, moment_layer, workers)
    return (new_params[None], new_first[None], new_second[None], new_fragment, new_momentum)


def solution(mesh):
    workers = mesh.shape["replica"]
    devices = mesh.devices.reshape(workers, XL, YN, CORES, XH)
    split = Mesh(devices, ("z", "xl", "y", "c", "xh"))
    fsdp = ("xl", "y", "c")
    return jax.shard_map(
        on_device,
        mesh=split,
        in_specs=(
            P(("z",) + fsdp, None),
            P(),
            P(("z",) + fsdp, "xh"),
            P("z", fsdp, "xh"),
            P("z", fsdp, "xh"),
            P("z", fsdp, "xh"),
            P("z", None, fsdp, "xh"),
            P(None, fsdp, "xh"),
            P(None, fsdp, "xh"),
            P(),
        ),
        out_specs=(
            P("z", fsdp, "xh"),
            P("z", fsdp, "xh"),
            P("z", fsdp, "xh"),
            P(fsdp, "xh"),
            P(fsdp, "xh"),
        ),
        check_vma=False,
    )
```

```python
import jax
import jax.numpy as jnp
from jax import lax
from jax.experimental import pallas as pl
from jax.experimental.pallas import tpu as pltpu
from jax.sharding import Mesh, PartitionSpec as P

NORM_EPS = 1e-05
CLIP_RMS = 8.0
FIRST_BETA = 0.9
SECOND_BETA = 0.95
FIRST_FIX = 1.0 - 0.9**10
SECOND_FIX = 1.0 - 0.95**10
ADAM_EPS = 1e-08
INNER_RATE = 0.01
DECAY_WEIGHT = 0.1
OUTER_RATE = 0.7
OUTER_BETA = 0.9

XL, YN, CORES, XH = 4, 8, 2, 2
PEERS = XL * YN * CORES * XH
TOK, COLS, FEAT = 128, 256, 128
HALF = XL * YN * FEAT
WIDE = HALF * CORES
HC = COLS // 2
NORM_ROWS = 32
CHIP_SCALE = 2.0**-8
X_SCALE = 2.0**-10
Y_SCALE = 2.0**-11
VMEM_BYTES = 24 * 2**20


def outer_update(summed, global_layer, moment_layer, workers):
    pseudo = global_layer - summed / workers
    new_momentum = OUTER_BETA * moment_layer + pseudo
    new_fragment = global_layer - OUTER_RATE * (pseudo + OUTER_BETA * new_momentum)
    return (new_fragment, new_momentum)


def norm_kernel(place, hidden, gain, cot, keep, send):
    send[:, HALF:] = cot[...]
    widened = hidden[...].astype(jnp.float32)
    mean_square = jnp.sum(widened * widened, axis=1, keepdims=True) * (1.0 / WIDE)
    inverse = lax.rsqrt(mean_square + NORM_EPS)
    first_core = place[1] == 0
    for block in range(XL * YN):
        pair = []
        for core in range(CORES):
            at = (block * CORES + core) * FEAT
            part = hidden[:, at : at + FEAT].astype(jnp.float32)
            scale = gain[at : at + FEAT].astype(jnp.float32)[None, :]
            pair.append((part * inverse * scale).astype(jnp.bfloat16))
        out = slice(block * FEAT, (block + 1) * FEAT)
        keep[:, out] = jnp.where(first_core, pair[0], pair[1])
        send[:, out] = jnp.where(first_core, pair[1], pair[0])


def split_norm(place, hidden_in, norm_gain, cot):
    def rows(width):
        return pl.BlockSpec((NORM_ROWS, width), lambda i, place: (i, 0))

    return pl.pallas_call(
        norm_kernel,
        grid_spec=pltpu.PrefetchScalarGridSpec(
            num_scalar_prefetch=1,
            grid=(TOK // NORM_ROWS,),
            in_specs=[
                rows(WIDE),
                pl.BlockSpec((WIDE,), lambda i, place: (0,)),
                rows(COLS),
            ],
            out_specs=[rows(HALF), rows(HALF + COLS)],
        ),
        out_shape=[
            pltpu.HBM((TOK, HALF), jnp.bfloat16),
            pltpu.HBM((TOK, HALF + COLS), jnp.bfloat16),
        ],
        cost_estimate=pl.CostEstimate(
            flops=8 * TOK * WIDE, bytes_accessed=4 * TOK * WIDE, transcendentals=TOK
        ),
        compiler_params=pltpu.CompilerParams(vmem_limit_bytes=VMEM_BYTES),
        name="split_norm",
    )(place, hidden_in, norm_gain, cot)


def partial_kernel(place, keep, recv, cot, other_cot, x_out, y_out, turned):
    @pl.when(pl.program_id(0) == 0)
    def _():
        turned[:, :TOK] = cot[...].T
        turned[:, TOK:] = other_cot[...].T

    contract = (((1,), (0,)), ((), ()))
    product = lax.dot_general(
        turned[:, :TOK], keep[...], contract, preferred_element_type=jnp.float32
    ) + lax.dot_general(
        turned[:, TOK:], recv[...], contract, preferred_element_type=jnp.float32
    )
    product = product * CHIP_SCALE
    for row in range(YN):
        block = product[:, row * FEAT : (row + 1) * FEAT]
        x_out[0, row] = block[:HC]
        y_out[row, 0] = block[HC:]


def chip_partial(place, keep, recv, cot):
    chunk = pl.BlockSpec((TOK, YN * FEAT), lambda k, place: (0, place[0] ^ k))
    mine = pl.BlockSpec((TOK, COLS), lambda k, place: (0, 0))
    other = pl.BlockSpec((TOK, COLS), lambda k, place: (0, HALF // COLS))
    return pl.pallas_call(
        partial_kernel,
        grid_spec=pltpu.PrefetchScalarGridSpec(
            num_scalar_prefetch=1,
            grid=(XL,),
            in_specs=[chunk, chunk, mine, other],
            out_specs=[
                pl.BlockSpec((1, YN, HC, FEAT), lambda k, place: (k, 0, 0, 0)),
                pl.BlockSpec((YN, 1, HC, FEAT), lambda k, place: (0, k, 0, 0)),
            ],
            scratch_shapes=[pltpu.VMEM((COLS, CORES * TOK), jnp.bfloat16)],
        ),
        out_shape=[
            jax.ShapeDtypeStruct((XL, YN, HC, FEAT), jnp.float32),
            jax.ShapeDtypeStruct((YN, XL, HC, FEAT), jnp.float32),
        ],
        cost_estimate=pl.CostEstimate(
            flops=4 * TOK * HALF * COLS, bytes_accessed=6 * 2**20, transcendentals=0
        ),
        compiler_params=pltpu.CompilerParams(vmem_limit_bytes=VMEM_BYTES),
        name="chip_partial",
    )(place, keep, recv, cot, recv)


def square_kernel(top, bottom, gradient, rows):
    upper, lower = top[...] * (1.0 / X_SCALE), bottom[...] * (1.0 / Y_SCALE)
    gradient[:, :HC] = upper.T
    gradient[:, HC:] = lower.T
    total = jnp.sum(upper * upper + lower * lower)
    rows[...] = jnp.full(rows.shape, total, jnp.float32)


def turn_and_square(top, bottom):
    return pl.pallas_call(
        square_kernel,
        in_specs=[pl.BlockSpec(memory_space=pltpu.VMEM)] * 2,
        out_specs=[pl.BlockSpec(memory_space=pltpu.VMEM)] * 2,
        out_shape=[
            jax.ShapeDtypeStruct((FEAT, COLS), jnp.float32),
            jax.ShapeDtypeStruct((PEERS, 1, 128), jnp.float32),
        ],
        cost_estimate=pl.CostEstimate(
            flops=4 * FEAT * COLS, bytes_accessed=2**18, transcendentals=0
        ),
        name="turn_and_square",
    )(top, bottom)


def update_kernel(rows, gradient, params, first, second, out_params, out_first, out_second):
    total_square = jnp.sum(jnp.sum(rows[...], axis=0), axis=1, keepdims=True) * (1.0 / 128)
    entries = FEAT * COLS * PEERS
    factor = jnp.minimum(1.0, CLIP_RMS * lax.rsqrt(total_square * (1.0 / entries) + 1e-06))
    clipped = factor * gradient[...]
    old = params[0]
    new_first = FIRST_BETA * first[0] + (1.0 - FIRST_BETA) * clipped
    new_second = SECOND_BETA * second[0] + (1.0 - SECOND_BETA) * clipped * clipped
    direction = new_first * (1.0 / FIRST_FIX) / (
        jnp.sqrt(new_second * (1.0 / SECOND_FIX)) + ADAM_EPS
    )
    out_params[0] = old - INNER_RATE * (direction + DECAY_WEIGHT * old)
    out_first[0] = new_first
    out_second[0] = new_second


def inner_update(rows, gradient, params, first, second):
    vmem = pl.BlockSpec(memory_space=pltpu.VMEM)
    block = jax.ShapeDtypeStruct((1, FEAT, COLS), jnp.float32)
    return pl.pallas_call(
        update_kernel,
        in_specs=[vmem] * 5,
        out_specs=[vmem] * 3,
        out_shape=[block, block, block],
        cost_estimate=pl.CostEstimate(
            flops=16 * FEAT * COLS, bytes_accessed=2**20, transcendentals=2 * FEAT * COLS
        ),
        name="inner_update",
    )(rows, gradient, params, first, second)


def swap_x(block, k):
    return lax.ppermute(block, "xl", [(i, i ^ k) for i in range(XL)])


def add_replica(value, step):
    return value + lax.ppermute(value, "z", [(i, i ^ step) for i in range(8)])


def worker_gradient(hidden_in, norm_gain, key_cotangent, local_layer):
    place = jnp.stack([lax.axis_index("xl"), lax.axis_index("c")]).astype(jnp.int32)
    local_layer = add_replica(local_layer, 1)
    keep, send = split_norm(place, hidden_in, norm_gain, key_cotangent)
    recv = lax.ppermute(send, "c", [(0, 1), (1, 0)])
    recv, local_layer = lax.optimization_barrier((recv, local_layer))
    x_wide, y_wide = chip_partial(place, keep, recv, key_cotangent)

    y_parts = lax.all_to_all(y_wide.astype(jnp.float16), "y", 0, 0, tiled=True)
    x_parts = [x_wide[k].astype(jnp.float16) for k in range(1, XL)]
    x_parts, local_layer = lax.optimization_barrier((x_parts, local_layer))
    x_sum = x_wide[0]
    for k in range(1, XL):
        x_sum = x_sum + swap_x(x_parts[k - 1], k).astype(jnp.float32)
    summed = add_replica(local_layer, 2)
    x_sum = (x_sum * (X_SCALE / CHIP_SCALE)).astype(jnp.float16)
    x_sum, y_parts, summed = lax.optimization_barrier((x_sum, y_parts, summed))
    y_sum = jnp.sum(y_parts.astype(jnp.float32) * (Y_SCALE / CHIP_SCALE), axis=0)

    top = lax.all_to_all(x_sum, "y", 0, 0, tiled=True)
    bottom = y_sum[0]
    for k in range(1, XL):
        bottom = bottom + swap_x(y_sum[k].astype(jnp.float16), k).astype(jnp.float32)
    top = jnp.sum(top.astype(jnp.float32), axis=0)
    return top, bottom, add_replica(summed, 4)


def on_device(
    hidden_in,
    norm_gain,
    key_cotangent,
    inner_params,
    inner_first,
    inner_second,
    frag_local,
    frag_global,
    outer_momentum,
    frag_index,
):
    layer_index = frag_index[0]
    local_layer = lax.dynamic_index_in_dim(frag_local[0], layer_index, 0, keepdims=False)
    top, bottom, summed = worker_gradient(hidden_in, norm_gain, key_cotangent, local_layer)
    gradient, rows = turn_and_square(top, bottom)
    rows = lax.all_to_all(rows, ("xl", "y", "c", "xh"), 0, 0, tiled=True)
    new_params, new_first, new_second = inner_update(
        rows, gradient, inner_params, inner_first, inner_second
    )

    global_layer = lax.dynamic_index_in_dim(frag_global, layer_index, 0, keepdims=False)
    moment_layer = lax.dynamic_index_in_dim(outer_momentum, layer_index, 0, keepdims=False)
    workers = lax.axis_size("z")
    new_fragment, new_momentum = outer_update(summed, global_layer, moment_layer, workers)
    return (new_params, new_first, new_second, new_fragment, new_momentum)


def solution(mesh):
    workers = mesh.shape["replica"]
    devices = mesh.devices.reshape(workers, XL, YN, CORES, XH)
    split = Mesh(devices, ("z", "xl", "y", "c", "xh"))
    fsdp = ("xl", "y", "c")
    return jax.shard_map(
        on_device,
        mesh=split,
        in_specs=(
            P(("z",) + fsdp, None),
            P(),
            P(("z",) + fsdp, "xh"),
            P("z", fsdp, "xh"),
            P("z", fsdp, "xh"),
            P("z", fsdp, "xh"),
            P("z", None, fsdp, "xh"),
            P(None, fsdp, "xh"),
            P(None, fsdp, "xh"),
            P(),
        ),
        out_specs=(
            P("z", fsdp, "xh"),
            P("z", fsdp, "xh"),
            P("z", fsdp, "xh"),
            P(fsdp, "xh"),
            P(fsdp, "xh"),
        ),
        check_vma=False,
    )
```

```python
import functools

import jax
import jax.numpy as jnp
from jax import lax
from jax.experimental import pallas as pl
from jax.experimental.pallas import tpu as pltpu
from jax.sharding import Mesh, PartitionSpec as P

NORM_EPS = 1e-05
CLIP_RMS = 8.0
FIRST_BETA = 0.9
SECOND_BETA = 0.95
FIRST_FIX = 1.0 - 0.9**10
SECOND_FIX = 1.0 - 0.95**10
ADAM_EPS = 1e-08
INNER_RATE = 0.01
DECAY_WEIGHT = 0.1
OUTER_RATE = 0.7
OUTER_BETA = 0.9

XL, YN, CORES, XH = 4, 8, 2, 2
PEERS = XL * YN * CORES * XH
TOK, COLS, FEAT = 128, 256, 128
HALF = XL * YN * FEAT
WIDE = HALF * CORES
HC = COLS // 2
NORM_ROWS = 32
CHIP_SCALE = 2.0**-8
X_SCALE = 2.0**-10
Y_SCALE = 2.0**-11
VMEM_BYTES = 24 * 2**20


def outer_update(summed, global_layer, moment_layer, workers):
    pseudo = global_layer - summed / workers
    new_momentum = OUTER_BETA * moment_layer + pseudo
    new_fragment = global_layer - OUTER_RATE * (pseudo + OUTER_BETA * new_momentum)
    return (new_fragment, new_momentum)


def norm_kernel(place, hidden, gain, cot, keep, send):
    send[:, HALF:] = cot[...]
    widened = hidden[...].astype(jnp.float32)
    mean_square = jnp.sum(widened * widened, axis=1, keepdims=True) * (1.0 / WIDE)
    inverse = lax.rsqrt(mean_square + NORM_EPS)
    first_core = place[1] == 0
    for block in range(XL * YN):
        pair = []
        for core in range(CORES):
            at = (block * CORES + core) * FEAT
            part = hidden[:, at : at + FEAT].astype(jnp.float32)
            scale = gain[at : at + FEAT].astype(jnp.float32)[None, :]
            pair.append((part * inverse * scale).astype(jnp.bfloat16))
        out = slice(block * FEAT, (block + 1) * FEAT)
        keep[:, out] = jnp.where(first_core, pair[0], pair[1])
        send[:, out] = jnp.where(first_core, pair[1], pair[0])


def split_norm(place, hidden_in, norm_gain, cot):
    def rows(width):
        return pl.BlockSpec((NORM_ROWS, width), lambda i, place: (i, 0))

    return pl.pallas_call(
        norm_kernel,
        grid_spec=pltpu.PrefetchScalarGridSpec(
            num_scalar_prefetch=1,
            grid=(TOK // NORM_ROWS,),
            in_specs=[
                rows(WIDE),
                pl.BlockSpec((WIDE,), lambda i, place: (0,)),
                rows(COLS),
            ],
            out_specs=[rows(HALF), rows(HALF + COLS)],
        ),
        out_shape=[
            pltpu.HBM((TOK, HALF), jnp.bfloat16),
            pltpu.HBM((TOK, HALF + COLS), jnp.bfloat16),
        ],
        cost_estimate=pl.CostEstimate(
            flops=8 * TOK * WIDE, bytes_accessed=4 * TOK * WIDE, transcendentals=TOK
        ),
        compiler_params=pltpu.CompilerParams(vmem_limit_bytes=VMEM_BYTES),
        name="split_norm",
    )(place, hidden_in, norm_gain, cot)


def partial_kernel(place, keep, recv, cot, other_cot, x_out, y_out, turned):
    @pl.when(pl.program_id(0) == 0)
    def _():
        turned[:, :TOK] = cot[...].T
        turned[:, TOK:] = other_cot[...].T

    contract = (((1,), (0,)), ((), ()))
    product = lax.dot_general(
        turned[:, :TOK], keep[...], contract, preferred_element_type=jnp.float32
    ) + lax.dot_general(
        turned[:, TOK:], recv[...], contract, preferred_element_type=jnp.float32
    )
    product = product * CHIP_SCALE
    for row in range(YN):
        block = product[:, row * FEAT : (row + 1) * FEAT]
        x_out[0, row] = block[:HC]
        y_out[row, 0] = block[HC:]


def chip_partial(place, keep, recv, cot):
    chunk = pl.BlockSpec((TOK, YN * FEAT), lambda k, place: (0, place[0] ^ k))
    mine = pl.BlockSpec((TOK, COLS), lambda k, place: (0, 0))
    other = pl.BlockSpec((TOK, COLS), lambda k, place: (0, HALF // COLS))
    return pl.pallas_call(
        partial_kernel,
        grid_spec=pltpu.PrefetchScalarGridSpec(
            num_scalar_prefetch=1,
            grid=(XL,),
            in_specs=[chunk, chunk, mine, other],
            out_specs=[
                pl.BlockSpec((1, YN, HC, FEAT), lambda k, place: (k, 0, 0, 0)),
                pl.BlockSpec((YN, 1, HC, FEAT), lambda k, place: (0, k, 0, 0)),
            ],
            scratch_shapes=[pltpu.VMEM((COLS, CORES * TOK), jnp.bfloat16)],
        ),
        out_shape=[
            jax.ShapeDtypeStruct((XL, YN, HC, FEAT), jnp.float32),
            jax.ShapeDtypeStruct((YN, XL, HC, FEAT), jnp.float32),
        ],
        cost_estimate=pl.CostEstimate(
            flops=4 * TOK * HALF * COLS, bytes_accessed=6 * 2**20, transcendentals=0
        ),
        compiler_params=pltpu.CompilerParams(vmem_limit_bytes=VMEM_BYTES),
        name="chip_partial",
    )(place, keep, recv, cot, recv)


def square_kernel(top, bottom, gradient, rows):
    upper, lower = top[...] * (1.0 / X_SCALE), bottom[...] * (1.0 / Y_SCALE)
    gradient[:, :HC] = upper.T
    gradient[:, HC:] = lower.T
    total = jnp.sum(upper * upper + lower * lower)
    rows[...] = jnp.full(rows.shape, total, jnp.float32)


def turn_and_square(top, bottom):
    return pl.pallas_call(
        square_kernel,
        in_specs=[pl.BlockSpec(memory_space=pltpu.VMEM)] * 2,
        out_specs=[pl.BlockSpec(memory_space=pltpu.VMEM)] * 2,
        out_shape=[
            jax.ShapeDtypeStruct((FEAT, COLS), jnp.float32),
            jax.ShapeDtypeStruct((PEERS, 1, 128), jnp.float32),
        ],
        cost_estimate=pl.CostEstimate(
            flops=4 * FEAT * COLS, bytes_accessed=2**18, transcendentals=0
        ),
        name="turn_and_square",
    )(top, bottom)


def update_kernel(rows, gradient, params, first, second, out_params, out_first, out_second):
    total_square = jnp.sum(jnp.sum(rows[...], axis=0), axis=1, keepdims=True) * (1.0 / 128)
    entries = FEAT * COLS * PEERS
    factor = jnp.minimum(1.0, CLIP_RMS * lax.rsqrt(total_square * (1.0 / entries) + 1e-06))
    clipped = factor * gradient[...]
    old = params[0]
    new_first = FIRST_BETA * first[0] + (1.0 - FIRST_BETA) * clipped
    new_second = SECOND_BETA * second[0] + (1.0 - SECOND_BETA) * clipped * clipped
    direction = new_first * (1.0 / FIRST_FIX) / (
        jnp.sqrt(new_second * (1.0 / SECOND_FIX)) + ADAM_EPS
    )
    out_params[0] = old - INNER_RATE * (direction + DECAY_WEIGHT * old)
    out_first[0] = new_first
    out_second[0] = new_second


def inner_update(rows, gradient, params, first, second):
    vmem = pl.BlockSpec(memory_space=pltpu.VMEM)
    block = jax.ShapeDtypeStruct((1, FEAT, COLS), jnp.float32)
    return pl.pallas_call(
        update_kernel,
        in_specs=[vmem] * 5,
        out_specs=[vmem] * 3,
        out_shape=[block, block, block],
        cost_estimate=pl.CostEstimate(
            flops=16 * FEAT * COLS, bytes_accessed=2**20, transcendentals=2 * FEAT * COLS
        ),
        name="inner_update",
    )(rows, gradient, params, first, second)


def swap_x(block, k):
    return lax.ppermute(block, "xl", [(i, i ^ k) for i in range(XL)])


def add_replica(value, step):
    return value + lax.ppermute(value, "z", [(i, i ^ step) for i in range(8)])


def worker_gradient(hidden_in, norm_gain, key_cotangent, local_layer):
    place = jnp.stack([lax.axis_index("xl"), lax.axis_index("c")]).astype(jnp.int32)
    in_hbm = functools.partial(pltpu.with_memory_space_constraint, memory_space=pltpu.HBM)
    hidden_in, norm_gain, key_cotangent = map(in_hbm, (hidden_in, norm_gain, key_cotangent))
    far_layer = lax.ppermute(local_layer, "z", [(i, i ^ 4) for i in range(8)])
    keep, send = split_norm(place, hidden_in, norm_gain, key_cotangent)
    recv = lax.ppermute(send, "c", [(0, 1), (1, 0)])
    x_wide, y_wide = chip_partial(place, in_hbm(keep), recv, key_cotangent)

    y_half = y_wide.astype(jnp.float16)
    y_half, far_layer = lax.optimization_barrier((y_half, far_layer))
    y_parts = lax.all_to_all(y_half, "y", 0, 0, tiled=True)
    x_near = swap_x(x_wide[1].astype(jnp.float16), 1)
    local_layer = local_layer + far_layer
    x_near, local_layer = lax.optimization_barrier((x_near, local_layer))
    x_sum = x_wide[0] + x_near.astype(jnp.float32)
    for k in range(2, XL):
        x_sum = x_sum + swap_x(x_wide[k].astype(jnp.float16), k).astype(jnp.float32)
    summed = add_replica(add_replica(local_layer, 1), 2)
    x_sum = (x_sum * (X_SCALE / CHIP_SCALE)).astype(jnp.float16)
    x_sum, y_parts, summed = lax.optimization_barrier((x_sum, y_parts, summed))
    y_sum = jnp.sum(y_parts.astype(jnp.float32) * (Y_SCALE / CHIP_SCALE), axis=0)

    top = lax.all_to_all(x_sum, "y", 0, 0, tiled=True)
    bottom = y_sum[0]
    for k in range(1, XL):
        bottom = bottom + swap_x(y_sum[k].astype(jnp.float16), k).astype(jnp.float32)
    top = jnp.sum(top.astype(jnp.float32), axis=0)
    return top, bottom, summed


def on_device(
    hidden_in,
    norm_gain,
    key_cotangent,
    inner_params,
    inner_first,
    inner_second,
    frag_local,
    frag_global,
    outer_momentum,
    frag_index,
):
    layer_index = frag_index[0]
    local_layer = lax.dynamic_index_in_dim(frag_local[0], layer_index, 0, keepdims=False)
    top, bottom, summed = worker_gradient(hidden_in, norm_gain, key_cotangent, local_layer)
    gradient, rows = turn_and_square(top, bottom)
    rows = lax.all_to_all(rows, ("xl", "y", "c", "xh"), 0, 0, tiled=True)
    new_params, new_first, new_second = inner_update(
        rows, gradient, inner_params, inner_first, inner_second
    )

    global_layer = lax.dynamic_index_in_dim(frag_global, layer_index, 0, keepdims=False)
    moment_layer = lax.dynamic_index_in_dim(outer_momentum, layer_index, 0, keepdims=False)
    workers = lax.axis_size("z")
    new_fragment, new_momentum = outer_update(summed, global_layer, moment_layer, workers)
    return (new_params, new_first, new_second, new_fragment, new_momentum)


def solution(mesh):
    workers = mesh.shape["replica"]
    devices = mesh.devices.reshape(workers, XL, YN, CORES, XH)
    split = Mesh(devices, ("z", "xl", "y", "c", "xh"))
    fsdp = ("xl", "y", "c")
    return jax.shard_map(
        on_device,
        mesh=split,
        in_specs=(
            P(("z",) + fsdp, None),
            P(),
            P(("z",) + fsdp, "xh"),
            P("z", fsdp, "xh"),
            P("z", fsdp, "xh"),
            P("z", fsdp, "xh"),
            P("z", None, fsdp, "xh"),
            P(None, fsdp, "xh"),
            P(None, fsdp, "xh"),
            P(),
        ),
        out_specs=(
            P("z", fsdp, "xh"),
            P("z", fsdp, "xh"),
            P("z", fsdp, "xh"),
            P(fsdp, "xh"),
            P(fsdp, "xh"),
        ),
        check_vma=False,
    )
```

```python
import functools

import jax
import jax.numpy as jnp
from jax import lax
from jax.experimental import pallas as pl
from jax.experimental.pallas import tpu as pltpu
from jax.sharding import Mesh, PartitionSpec as P

NORM_EPS = 1e-05
CLIP_RMS = 8.0
FIRST_BETA = 0.9
SECOND_BETA = 0.95
FIRST_FIX = 1.0 - 0.9**10
SECOND_FIX = 1.0 - 0.95**10
ADAM_EPS = 1e-08
INNER_RATE = 0.01
DECAY_WEIGHT = 0.1
OUTER_RATE = 0.7
OUTER_BETA = 0.9

XL, YN, CORES, XH = 4, 8, 2, 2
PEERS = XL * YN * CORES * XH
TOK, COLS, FEAT = 128, 256, 128
HALF = XL * YN * FEAT
WIDE = HALF * CORES
HC = COLS // 2
NORM_ROWS = 16
STEP_ROWS = 4
CHIP_SCALE = 2.0**-8
X_SCALE = 2.0**-10
Y_SCALE = 2.0**-12
VMEM_BYTES = 24 * 2**20


def outer_update(summed, global_layer, moment_layer, workers):
    pseudo = global_layer - summed / workers
    new_momentum = OUTER_BETA * moment_layer + pseudo
    new_fragment = global_layer - OUTER_RATE * (pseudo + OUTER_BETA * new_momentum)
    return (new_fragment, new_momentum)


def norm_kernel(place, hidden, gain, cot, keep, send):
    send[:, HALF:] = cot[...]
    widened = hidden[...].astype(jnp.float32)
    mean_square = jnp.sum(widened * widened, axis=1, keepdims=True) * (1.0 / WIDE)
    inverse = lax.rsqrt(mean_square + NORM_EPS)
    first_core = place[1] == 0
    for block in range(XL * YN):
        pair = []
        for core in range(CORES):
            at = (block * CORES + core) * FEAT
            part = hidden[:, at : at + FEAT].astype(jnp.float32)
            scale = gain[at : at + FEAT].astype(jnp.float32)[None, :]
            pair.append((part * inverse * scale).astype(jnp.bfloat16))
        out = slice(block * FEAT, (block + 1) * FEAT)
        keep[:, out] = jnp.where(first_core, pair[0], pair[1])
        send[:, out] = jnp.where(first_core, pair[1], pair[0])


def split_norm(place, hidden_in, norm_gain, cot):
    def rows(width):
        return pl.BlockSpec((NORM_ROWS, width), lambda i, place: (i, 0))

    return pl.pallas_call(
        norm_kernel,
        grid_spec=pltpu.PrefetchScalarGridSpec(
            num_scalar_prefetch=1,
            grid=(TOK // NORM_ROWS,),
            in_specs=[
                rows(WIDE),
                pl.BlockSpec((WIDE,), lambda i, place: (0,)),
                rows(COLS),
            ],
            out_specs=[rows(HALF), rows(HALF + COLS)],
        ),
        out_shape=[
            pltpu.HBM((TOK, HALF), jnp.bfloat16),
            pltpu.HBM((TOK, HALF + COLS), jnp.bfloat16),
        ],
        cost_estimate=pl.CostEstimate(
            flops=8 * TOK * WIDE, bytes_accessed=4 * TOK * WIDE, transcendentals=TOK
        ),
        compiler_params=pltpu.CompilerParams(vmem_limit_bytes=VMEM_BYTES),
        name="split_norm",
    )(place, hidden_in, norm_gain, cot)


def partial_kernel(place, keep, recv, cot, other_cot, x_out, y_out, turned):
    @pl.when((pl.program_id(0) == 0) & (pl.program_id(1) == 0))
    def _():
        turned[:, :TOK] = cot[...].T
        turned[:, TOK:] = other_cot[...].T

    contract = (((1,), (0,)), ((), ()))
    product = lax.dot_general(
        turned[:, :TOK], keep[...], contract, preferred_element_type=jnp.float32
    ) + lax.dot_general(
        turned[:, TOK:], recv[...], contract, preferred_element_type=jnp.float32
    )
    product = product * CHIP_SCALE
    for row in range(STEP_ROWS):
        block = product[:, row * FEAT : (row + 1) * FEAT]
        x_out[0, row] = block[:HC]
        y_out[0, row, 0] = block[HC:]


def chip_partial(place, keep, recv, cot):
    steps = YN // STEP_ROWS
    chunk = pl.BlockSpec(
        (TOK, STEP_ROWS * FEAT), lambda k, h, place: (0, (place[0] ^ k) * steps + h)
    )
    mine = pl.BlockSpec((TOK, COLS), lambda k, h, place: (0, 0))
    other = pl.BlockSpec((TOK, COLS), lambda k, h, place: (0, HALF // COLS))
    return pl.pallas_call(
        partial_kernel,
        grid_spec=pltpu.PrefetchScalarGridSpec(
            num_scalar_prefetch=1,
            grid=(XL, steps),
            in_specs=[chunk, chunk, mine, other],
            out_specs=[
                pl.BlockSpec((1, STEP_ROWS, HC, FEAT), lambda k, h, place: (k, h, 0, 0)),
                pl.BlockSpec(
                    (1, STEP_ROWS, 1, HC, FEAT),
                    lambda k, h, place: ((place[0] ^ k) & 1, h, k // 2, 0, 0),
                ),
            ],
            scratch_shapes=[pltpu.VMEM((COLS, CORES * TOK), jnp.bfloat16)],
        ),
        out_shape=[
            jax.ShapeDtypeStruct((XL, YN, HC, FEAT), jnp.float32),
            jax.ShapeDtypeStruct((XL // 2, YN, 2, HC, FEAT), jnp.float32),
        ],
        cost_estimate=pl.CostEstimate(
            flops=4 * TOK * HALF * COLS, bytes_accessed=6 * 2**20, transcendentals=0
        ),
        compiler_params=pltpu.CompilerParams(vmem_limit_bytes=VMEM_BYTES),
        name="chip_partial",
    )(place, keep, recv, cot, recv)


def square_kernel(top, bottom, gradient, rows):
    upper, lower = top[...] * (1.0 / X_SCALE), bottom[...] * (1.0 / Y_SCALE)
    gradient[:, :HC] = upper.T
    gradient[:, HC:] = lower.T
    total = jnp.sum(upper * upper + lower * lower)
    rows[...] = jnp.full(rows.shape, total, jnp.float32)


def turn_and_square(top, bottom):
    return pl.pallas_call(
        square_kernel,
        in_specs=[pl.BlockSpec(memory_space=pltpu.VMEM)] * 2,
        out_specs=[pl.BlockSpec(memory_space=pltpu.VMEM)] * 2,
        out_shape=[
            jax.ShapeDtypeStruct((FEAT, COLS), jnp.float32),
            jax.ShapeDtypeStruct((PEERS, 1, 128), jnp.float32),
        ],
        cost_estimate=pl.CostEstimate(
            flops=4 * FEAT * COLS, bytes_accessed=2**18, transcendentals=0
        ),
        name="turn_and_square",
    )(top, bottom)


def update_kernel(rows, gradient, params, first, second, out_params, out_first, out_second):
    total_square = jnp.sum(jnp.sum(rows[...], axis=0), axis=1, keepdims=True) * (1.0 / 128)
    entries = FEAT * COLS * PEERS
    factor = jnp.minimum(1.0, CLIP_RMS * lax.rsqrt(total_square * (1.0 / entries) + 1e-06))
    clipped = factor * gradient[...]
    old = params[0]
    new_first = FIRST_BETA * first[0] + (1.0 - FIRST_BETA) * clipped
    new_second = SECOND_BETA * second[0] + (1.0 - SECOND_BETA) * clipped * clipped
    direction = new_first * (1.0 / FIRST_FIX) / (
        jnp.sqrt(new_second * (1.0 / SECOND_FIX)) + ADAM_EPS
    )
    out_params[0] = old - INNER_RATE * (direction + DECAY_WEIGHT * old)
    out_first[0] = new_first
    out_second[0] = new_second


def inner_update(rows, gradient, params, first, second):
    vmem = pl.BlockSpec(memory_space=pltpu.VMEM)
    block = jax.ShapeDtypeStruct((1, FEAT, COLS), jnp.float32)
    return pl.pallas_call(
        update_kernel,
        in_specs=[vmem] * 5,
        out_specs=[vmem] * 3,
        out_shape=[block, block, block],
        cost_estimate=pl.CostEstimate(
            flops=16 * FEAT * COLS, bytes_accessed=2**20, transcendentals=2 * FEAT * COLS
        ),
        name="inner_update",
    )(rows, gradient, params, first, second)


def swap_x(block, k):
    return lax.ppermute(block, ("xp", "xb"), [(i, i ^ k) for i in range(XL)])


def add_replica(value, step):
    return value + lax.ppermute(value, "z", [(i, i ^ step) for i in range(8)])


def worker_gradient(hidden_in, norm_gain, key_cotangent, local_layer):
    place = jnp.stack([lax.axis_index(("xp", "xb")), lax.axis_index("c")]).astype(jnp.int32)
    in_hbm = functools.partial(pltpu.with_memory_space_constraint, memory_space=pltpu.HBM)
    hidden_in, norm_gain, key_cotangent = map(in_hbm, (hidden_in, norm_gain, key_cotangent))
    far_layer = lax.ppermute(local_layer, "z", [(i, i ^ 4) for i in range(8)])
    keep, send = split_norm(place, hidden_in, norm_gain, key_cotangent)
    recv = lax.ppermute(send, "c", [(0, 1), (1, 0)])
    x_wide, y_wide = chip_partial(place, in_hbm(keep), recv, key_cotangent)

    y_half = y_wide.astype(jnp.float16).reshape(YN * XL // 2, 2, HC, FEAT)
    y_half, far_layer = lax.optimization_barrier((y_half, far_layer))
    y_parts = lax.all_to_all(y_half, ("xb", "y"), 0, 0, tiled=True)
    x_near = swap_x(x_wide[1].astype(jnp.float16), 1)
    local_layer = local_layer + far_layer
    x_near, local_layer = lax.optimization_barrier((x_near, local_layer))
    x_sum = x_wide[0] + x_near.astype(jnp.float32)
    for k in range(2, XL):
        x_sum = x_sum + swap_x(x_wide[k].astype(jnp.float16), k).astype(jnp.float32)
    summed = add_replica(add_replica(local_layer, 1), 2)
    x_sum = (x_sum * (X_SCALE / CHIP_SCALE)).astype(jnp.float16)
    x_sum, y_parts, summed = lax.optimization_barrier((x_sum, y_parts, summed))
    y_sum = jnp.sum(y_parts.astype(jnp.float32) * (Y_SCALE / CHIP_SCALE), axis=0)

    top = lax.all_to_all(x_sum, "y", 0, 0, tiled=True)
    bottom = y_sum[0] + swap_x(y_sum[1].astype(jnp.float16), 2).astype(jnp.float32)
    top = jnp.sum(top.astype(jnp.float32), axis=0)
    return top, bottom, summed


def on_device(
    hidden_in,
    norm_gain,
    key_cotangent,
    inner_params,
    inner_first,
    inner_second,
    frag_local,
    frag_global,
    outer_momentum,
    frag_index,
):
    layer_index = frag_index[0]
    local_layer = lax.dynamic_index_in_dim(frag_local[0], layer_index, 0, keepdims=False)
    top, bottom, summed = worker_gradient(hidden_in, norm_gain, key_cotangent, local_layer)
    gradient, rows = turn_and_square(top, bottom)
    rows = lax.all_to_all(rows, ("xp", "xb", "y", "c", "xh"), 0, 0, tiled=True)
    new_params, new_first, new_second = inner_update(
        rows, gradient, inner_params, inner_first, inner_second
    )

    global_layer = lax.dynamic_index_in_dim(frag_global, layer_index, 0, keepdims=False)
    moment_layer = lax.dynamic_index_in_dim(outer_momentum, layer_index, 0, keepdims=False)
    workers = lax.axis_size("z")
    new_fragment, new_momentum = outer_update(summed, global_layer, moment_layer, workers)
    return (new_params, new_first, new_second, new_fragment, new_momentum)


def solution(mesh):
    workers = mesh.shape["replica"]
    devices = mesh.devices.reshape(workers, XL // 2, 2, YN, CORES, XH)
    split = Mesh(devices, ("z", "xp", "xb", "y", "c", "xh"))
    fsdp = ("xp", "xb", "y", "c")
    return jax.shard_map(
        on_device,
        mesh=split,
        in_specs=(
            P(("z",) + fsdp, None),
            P(),
            P(("z",) + fsdp, "xh"),
            P("z", fsdp, "xh"),
            P("z", fsdp, "xh"),
            P("z", fsdp, "xh"),
            P("z", None, fsdp, "xh"),
            P(None, fsdp, "xh"),
            P(None, fsdp, "xh"),
            P(),
        ),
        out_specs=(
            P("z", fsdp, "xh"),
            P("z", fsdp, "xh"),
            P("z", fsdp, "xh"),
            P(fsdp, "xh"),
            P(fsdp, "xh"),
        ),
        check_vma=False,
    )
```

```python
import functools

import jax
import jax.numpy as jnp
from jax import lax
from jax.experimental import pallas as pl
from jax.experimental.pallas import tpu as pltpu
from jax.sharding import Mesh, PartitionSpec as P

NORM_EPS = 1e-05
CLIP_RMS = 8.0
FIRST_BETA = 0.9
SECOND_BETA = 0.95
FIRST_FIX = 1.0 - 0.9**10
SECOND_FIX = 1.0 - 0.95**10
ADAM_EPS = 1e-08
INNER_RATE = 0.01
DECAY_WEIGHT = 0.1
OUTER_RATE = 0.7
OUTER_BETA = 0.9

XL, YN, CORES, XH = 4, 8, 2, 2
PEERS = XL * YN * CORES * XH
TOK, COLS, FEAT = 128, 256, 128
HALF = XL * YN * FEAT
WIDE = HALF * CORES
HC = COLS // 2
NORM_ROWS = 64
CHIP_SCALE = 2.0**-8
X_SCALE = 2.0**-10
Y_SCALE = 2.0**-12
VMEM_BYTES = 24 * 2**20


def outer_update(summed, global_layer, moment_layer, workers):
    pseudo = global_layer - summed / workers
    new_momentum = OUTER_BETA * moment_layer + pseudo
    new_fragment = global_layer - OUTER_RATE * (pseudo + OUTER_BETA * new_momentum)
    return (new_fragment, new_momentum)


def norm_kernel(place, hidden, gain, cot, keep, send):
    send[:, HALF:] = cot[...]
    widened = hidden[...].astype(jnp.float32)
    mean_square = jnp.sum(widened * widened, axis=1, keepdims=True) * (1.0 / WIDE)
    inverse = lax.rsqrt(mean_square + NORM_EPS)
    first_core = place[1] == 0
    for block in range(XL * YN):
        pair = []
        for core in range(CORES):
            at = (block * CORES + core) * FEAT
            part = hidden[:, at : at + FEAT].astype(jnp.float32)
            scale = gain[at : at + FEAT].astype(jnp.float32)[None, :]
            pair.append((part * inverse * scale).astype(jnp.bfloat16))
        out = slice(block * FEAT, (block + 1) * FEAT)
        keep[:, out] = jnp.where(first_core, pair[0], pair[1])
        send[:, out] = jnp.where(first_core, pair[1], pair[0])


def split_norm(place, hidden_in, norm_gain, cot):
    def rows(width):
        return pl.BlockSpec((NORM_ROWS, width), lambda i, place: (i, 0))

    return pl.pallas_call(
        norm_kernel,
        grid_spec=pltpu.PrefetchScalarGridSpec(
            num_scalar_prefetch=1,
            grid=(TOK // NORM_ROWS,),
            in_specs=[
                rows(WIDE),
                pl.BlockSpec((WIDE,), lambda i, place: (0,)),
                rows(COLS),
            ],
            out_specs=[rows(HALF), rows(HALF + COLS)],
        ),
        out_shape=[
            pltpu.HBM((TOK, HALF), jnp.bfloat16),
            pltpu.HBM((TOK, HALF + COLS), jnp.bfloat16),
        ],
        cost_estimate=pl.CostEstimate(
            flops=8 * TOK * WIDE, bytes_accessed=4 * TOK * WIDE, transcendentals=TOK
        ),
        compiler_params=pltpu.CompilerParams(vmem_limit_bytes=VMEM_BYTES),
        name="split_norm",
    )(place, hidden_in, norm_gain, cot)


def partial_kernel(place, keep, recv, cot, other_cot, x_out, y_out, turned):
    @pl.when(pl.program_id(0) == 0)
    def _():
        turned[:, :TOK] = cot[...].T
        turned[:, TOK:] = other_cot[...].T

    contract = (((1,), (0,)), ((), ()))
    width = YN * FEAT
    for near in range(2):
        dest = (place[0] ^ near) & 1
        chunk = pl.ds(pl.multiple_of(dest * width, width), width)
        product = lax.dot_general(
            turned[:, :TOK], keep[:, chunk], contract, preferred_element_type=jnp.float32
        ) + lax.dot_general(
            turned[:, TOK:], recv[:, chunk], contract, preferred_element_type=jnp.float32
        )
        product = product * CHIP_SCALE
        for row in range(YN):
            block = product[:, row * FEAT : (row + 1) * FEAT]
            x_out[near, row] = block[:HC]
            y_out[dest, row, 0] = block[HC:]


def chip_partial(place, keep, recv, cot):
    chunk = pl.BlockSpec((TOK, 2 * YN * FEAT), lambda far, place: (0, (place[0] // 2) ^ far))
    mine = pl.BlockSpec((TOK, COLS), lambda far, place: (0, 0))
    other = pl.BlockSpec((TOK, COLS), lambda far, place: (0, HALF // COLS))
    return pl.pallas_call(
        partial_kernel,
        grid_spec=pltpu.PrefetchScalarGridSpec(
            num_scalar_prefetch=1,
            grid=(XL // 2,),
            in_specs=[chunk, chunk, mine, other],
            out_specs=[
                pl.BlockSpec((2, YN, HC, FEAT), lambda far, place: (far, 0, 0, 0)),
                pl.BlockSpec((2, YN, 1, HC, FEAT), lambda far, place: (0, 0, far, 0, 0)),
            ],
            scratch_shapes=[pltpu.VMEM((COLS, CORES * TOK), jnp.bfloat16)],
        ),
        out_shape=[
            jax.ShapeDtypeStruct((XL, YN, HC, FEAT), jnp.float32),
            jax.ShapeDtypeStruct((XL // 2, YN, 2, HC, FEAT), jnp.float32),
        ],
        cost_estimate=pl.CostEstimate(
            flops=4 * TOK * HALF * COLS, bytes_accessed=6 * 2**20, transcendentals=0
        ),
        compiler_params=pltpu.CompilerParams(vmem_limit_bytes=VMEM_BYTES),
        name="chip_partial",
    )(place, keep, recv, cot, recv)


def square_kernel(top, bottom, gradient, rows):
    upper, lower = top[...] * (1.0 / X_SCALE), bottom[...] * (1.0 / Y_SCALE)
    gradient[:, :HC] = upper.T
    gradient[:, HC:] = lower.T
    total = jnp.sum(upper * upper + lower * lower)
    rows[...] = jnp.full(rows.shape, total, jnp.float32)


def turn_and_square(top, bottom):
    return pl.pallas_call(
        square_kernel,
        in_specs=[pl.BlockSpec(memory_space=pltpu.VMEM)] * 2,
        out_specs=[pl.BlockSpec(memory_space=pltpu.VMEM)] * 2,
        out_shape=[
            jax.ShapeDtypeStruct((FEAT, COLS), jnp.float32),
            jax.ShapeDtypeStruct((PEERS, 1, 128), jnp.float32),
        ],
        cost_estimate=pl.CostEstimate(
            flops=4 * FEAT * COLS, bytes_accessed=2**18, transcendentals=0
        ),
        name="turn_and_square",
    )(top, bottom)


def update_kernel(rows, gradient, params, first, second, out_params, out_first, out_second):
    total_square = jnp.sum(jnp.sum(rows[...], axis=0), axis=1, keepdims=True) * (1.0 / 128)
    entries = FEAT * COLS * PEERS
    factor = jnp.minimum(1.0, CLIP_RMS * lax.rsqrt(total_square * (1.0 / entries) + 1e-06))
    clipped = factor * gradient[...]
    old = params[0]
    new_first = FIRST_BETA * first[0] + (1.0 - FIRST_BETA) * clipped
    new_second = SECOND_BETA * second[0] + (1.0 - SECOND_BETA) * clipped * clipped
    direction = new_first * (1.0 / FIRST_FIX) / (
        jnp.sqrt(new_second * (1.0 / SECOND_FIX)) + ADAM_EPS
    )
    out_params[0] = old - INNER_RATE * (direction + DECAY_WEIGHT * old)
    out_first[0] = new_first
    out_second[0] = new_second


def inner_update(rows, gradient, params, first, second):
    vmem = pl.BlockSpec(memory_space=pltpu.VMEM)
    block = jax.ShapeDtypeStruct((1, FEAT, COLS), jnp.float32)
    return pl.pallas_call(
        update_kernel,
        in_specs=[vmem] * 5,
        out_specs=[vmem] * 3,
        out_shape=[block, block, block],
        cost_estimate=pl.CostEstimate(
            flops=16 * FEAT * COLS, bytes_accessed=2**20, transcendentals=2 * FEAT * COLS
        ),
        name="inner_update",
    )(rows, gradient, params, first, second)


def swap_x(block, k):
    return lax.ppermute(block, ("xp", "xb"), [(i, i ^ k) for i in range(XL)])


def add_replica(value, step):
    return value + lax.ppermute(value, "z", [(i, i ^ step) for i in range(8)])


def worker_gradient(hidden_in, norm_gain, key_cotangent, local_layer):
    place = jnp.stack([lax.axis_index(("xp", "xb")), lax.axis_index("c")]).astype(jnp.int32)
    in_hbm = functools.partial(pltpu.with_memory_space_constraint, memory_space=pltpu.HBM)
    hidden_in, norm_gain, key_cotangent = map(in_hbm, (hidden_in, norm_gain, key_cotangent))
    far_layer = lax.ppermute(local_layer, "z", [(i, i ^ 4) for i in range(8)])
    keep, send = split_norm(place, hidden_in, norm_gain, key_cotangent)
    recv = lax.ppermute(send, "c", [(0, 1), (1, 0)])
    x_wide, y_wide = chip_partial(place, in_hbm(keep), recv, key_cotangent)

    y_half = y_wide.astype(jnp.float16).reshape(YN * XL // 2, 2, HC, FEAT)
    y_half, far_layer = lax.optimization_barrier((y_half, far_layer))
    y_parts = lax.all_to_all(y_half, ("xb", "y"), 0, 0, tiled=True)
    local_layer = local_layer + far_layer
    x_sum = x_wide[0]
    for k in range(1, XL):
        x_sum = x_sum + swap_x(x_wide[k].astype(jnp.float16), k).astype(jnp.float32)
    summed = add_replica(local_layer, 1)
    x_sum = (x_sum * (X_SCALE / CHIP_SCALE)).astype(jnp.float16)
    x_sum, y_parts, summed = lax.optimization_barrier((x_sum, y_parts, summed))
    y_sum = jnp.sum(y_parts.astype(jnp.float32) * (Y_SCALE / CHIP_SCALE), axis=0)

    top = lax.all_to_all(x_sum, "y", 0, 0, tiled=True)
    bottom = y_sum[0] + swap_x(y_sum[1].astype(jnp.float16), 2).astype(jnp.float32)
    top = jnp.sum(top.astype(jnp.float32), axis=0)
    return top, bottom, add_replica(summed, 2)


def on_device(
    hidden_in,
    norm_gain,
    key_cotangent,
    inner_params,
    inner_first,
    inner_second,
    frag_local,
    frag_global,
    outer_momentum,
    frag_index,
):
    layer_index = frag_index[0]
    local_layer = lax.dynamic_index_in_dim(frag_local[0], layer_index, 0, keepdims=False)
    top, bottom, summed = worker_gradient(hidden_in, norm_gain, key_cotangent, local_layer)
    gradient, rows = turn_and_square(top, bottom)
    rows = lax.all_to_all(rows, ("xp", "xb", "y", "c", "xh"), 0, 0, tiled=True)
    new_params, new_first, new_second = inner_update(
        rows, gradient, inner_params, inner_first, inner_second
    )

    global_layer = lax.dynamic_index_in_dim(frag_global, layer_index, 0, keepdims=False)
    moment_layer = lax.dynamic_index_in_dim(outer_momentum, layer_index, 0, keepdims=False)
    workers = lax.axis_size("z")
    new_fragment, new_momentum = outer_update(summed, global_layer, moment_layer, workers)
    return (new_params, new_first, new_second, new_fragment, new_momentum)


def solution(mesh):
    workers = mesh.shape["replica"]
    devices = mesh.devices.reshape(workers, XL // 2, 2, YN, CORES, XH)
    split = Mesh(devices, ("z", "xp", "xb", "y", "c", "xh"))
    fsdp = ("xp", "xb", "y", "c")
    return jax.shard_map(
        on_device,
        mesh=split,
        in_specs=(
            P(("z",) + fsdp, None),
            P(),
            P(("z",) + fsdp, "xh"),
            P("z", fsdp, "xh"),
            P("z", fsdp, "xh"),
            P("z", fsdp, "xh"),
            P("z", None, fsdp, "xh"),
            P(None, fsdp, "xh"),
            P(None, fsdp, "xh"),
            P(),
        ),
        out_specs=(
            P("z", fsdp, "xh"),
            P("z", fsdp, "xh"),
            P("z", fsdp, "xh"),
            P(fsdp, "xh"),
            P(fsdp, "xh"),
        ),
        check_vma=False,
    )
```

```python
import functools

import jax
import jax.numpy as jnp
from jax import lax
from jax.experimental import pallas as pl
from jax.experimental.pallas import tpu as pltpu
from jax.sharding import Mesh, PartitionSpec as P

NORM_EPS = 1e-05
CLIP_RMS = 8.0
FIRST_BETA = 0.9
SECOND_BETA = 0.95
FIRST_FIX = 1.0 - 0.9**10
SECOND_FIX = 1.0 - 0.95**10
ADAM_EPS = 1e-08
INNER_RATE = 0.01
DECAY_WEIGHT = 0.1
OUTER_RATE = 0.7
OUTER_BETA = 0.9

XL, YN, CORES, XH = 4, 8, 2, 2
PEERS = XL * YN * CORES * XH
TOK, COLS, FEAT = 128, 256, 128
HALF = XL * YN * FEAT
WIDE = HALF * CORES
HC = COLS // 2
NORM_ROWS = 64
CHIP_SCALE = 2.0**-8
X_SCALE = 2.0**-10
Y_SCALE = 2.0**-12
VMEM_BYTES = 24 * 2**20


def outer_update(summed, global_layer, moment_layer, workers):
    pseudo = global_layer - summed / workers
    new_momentum = OUTER_BETA * moment_layer + pseudo
    new_fragment = global_layer - OUTER_RATE * (pseudo + OUTER_BETA * new_momentum)
    return (new_fragment, new_momentum)


def norm_kernel(place, hidden, gain, cot, keep, send):
    send[:, HALF:] = cot[...]
    widened = hidden[...].astype(jnp.float32)
    mean_square = jnp.sum(widened * widened, axis=1, keepdims=True) * (1.0 / WIDE)
    inverse = lax.rsqrt(mean_square + NORM_EPS)
    first_core = place[1] == 0
    for block in range(XL * YN):
        pair = []
        for core in range(CORES):
            at = (block * CORES + core) * FEAT
            part = hidden[:, at : at + FEAT].astype(jnp.float32)
            scale = gain[at : at + FEAT].astype(jnp.float32)[None, :]
            pair.append((part * inverse * scale).astype(jnp.bfloat16))
        out = slice(block * FEAT, (block + 1) * FEAT)
        keep[:, out] = jnp.where(first_core, pair[0], pair[1])
        send[:, out] = jnp.where(first_core, pair[1], pair[0])


def split_norm(place, hidden_in, norm_gain, cot):
    def rows(width):
        return pl.BlockSpec((NORM_ROWS, width), lambda i, place: (i, 0))

    return pl.pallas_call(
        norm_kernel,
        grid_spec=pltpu.PrefetchScalarGridSpec(
            num_scalar_prefetch=1,
            grid=(TOK // NORM_ROWS,),
            in_specs=[
                rows(WIDE),
                pl.BlockSpec((WIDE,), lambda i, place: (0,)),
                rows(COLS),
            ],
            out_specs=[rows(HALF), rows(HALF + COLS)],
        ),
        out_shape=[
            pltpu.HBM((TOK, HALF), jnp.bfloat16),
            pltpu.HBM((TOK, HALF + COLS), jnp.bfloat16),
        ],
        cost_estimate=pl.CostEstimate(
            flops=8 * TOK * WIDE, bytes_accessed=4 * TOK * WIDE, transcendentals=TOK
        ),
        compiler_params=pltpu.CompilerParams(vmem_limit_bytes=VMEM_BYTES),
        name="split_norm",
    )(place, hidden_in, norm_gain, cot)


def partial_kernel(place, keep, recv, cot, other_cot, x_out, y_out, turned):
    @pl.when(pl.program_id(0) == 0)
    def _():
        turned[:, :TOK] = cot[...].T
        turned[:, TOK:] = other_cot[...].T

    contract = (((1,), (0,)), ((), ()))
    width = YN * FEAT
    for near in range(2):
        dest = (place[0] ^ near) & 1
        chunk = pl.ds(pl.multiple_of(dest * width, width), width)
        product = lax.dot_general(
            turned[:, :TOK], keep[:, chunk], contract, preferred_element_type=jnp.float32
        ) + lax.dot_general(
            turned[:, TOK:], recv[:, chunk], contract, preferred_element_type=jnp.float32
        )
        product = product * CHIP_SCALE
        for row in range(YN):
            block = product[:, row * FEAT : (row + 1) * FEAT]
            x_out[near, row] = block[:HC]
            y_out[dest, row, 0] = block[HC:]


def chip_partial(place, keep, recv, cot):
    chunk = pl.BlockSpec((TOK, 2 * YN * FEAT), lambda far, place: (0, (place[0] // 2) ^ far))
    mine = pl.BlockSpec((TOK, COLS), lambda far, place: (0, 0))
    other = pl.BlockSpec((TOK, COLS), lambda far, place: (0, HALF // COLS))
    return pl.pallas_call(
        partial_kernel,
        grid_spec=pltpu.PrefetchScalarGridSpec(
            num_scalar_prefetch=1,
            grid=(XL // 2,),
            in_specs=[chunk, chunk, mine, other],
            out_specs=[
                pl.BlockSpec((2, YN, HC, FEAT), lambda far, place: (far, 0, 0, 0)),
                pl.BlockSpec((2, YN, 1, HC, FEAT), lambda far, place: (0, 0, far, 0, 0)),
            ],
            scratch_shapes=[pltpu.VMEM((COLS, CORES * TOK), jnp.bfloat16)],
        ),
        out_shape=[
            jax.ShapeDtypeStruct((XL, YN, HC, FEAT), jnp.float32),
            jax.ShapeDtypeStruct((XL // 2, YN, 2, HC, FEAT), jnp.float32),
        ],
        cost_estimate=pl.CostEstimate(
            flops=4 * TOK * HALF * COLS, bytes_accessed=6 * 2**20, transcendentals=0
        ),
        compiler_params=pltpu.CompilerParams(vmem_limit_bytes=VMEM_BYTES),
        name="chip_partial",
    )(place, keep, recv, cot, recv)


def square_kernel(top, bottom, gradient, rows):
    upper, lower = top[...] * (1.0 / X_SCALE), bottom[...] * (1.0 / Y_SCALE)
    gradient[:, :HC] = upper.T
    gradient[:, HC:] = lower.T
    total = jnp.sum(upper * upper + lower * lower)
    rows[...] = jnp.full(rows.shape, total, jnp.float32)


def turn_and_square(top, bottom):
    return pl.pallas_call(
        square_kernel,
        in_specs=[pl.BlockSpec(memory_space=pltpu.VMEM)] * 2,
        out_specs=[pl.BlockSpec(memory_space=pltpu.VMEM)] * 2,
        out_shape=[
            jax.ShapeDtypeStruct((FEAT, COLS), jnp.float32),
            jax.ShapeDtypeStruct((PEERS, 1, 128), jnp.float32),
        ],
        cost_estimate=pl.CostEstimate(
            flops=4 * FEAT * COLS, bytes_accessed=2**18, transcendentals=0
        ),
        name="turn_and_square",
    )(top, bottom)


def update_kernel(rows, gradient, params, first, second, out_params, out_first, out_second):
    total_square = jnp.sum(jnp.sum(rows[...], axis=0), axis=1, keepdims=True) * (1.0 / 128)
    entries = FEAT * COLS * PEERS
    factor = jnp.minimum(1.0, CLIP_RMS * lax.rsqrt(total_square * (1.0 / entries) + 1e-06))
    clipped = factor * gradient[...]
    old = params[0]
    new_first = FIRST_BETA * first[0] + (1.0 - FIRST_BETA) * clipped
    new_second = SECOND_BETA * second[0] + (1.0 - SECOND_BETA) * clipped * clipped
    direction = new_first * (1.0 / FIRST_FIX) / (
        jnp.sqrt(new_second * (1.0 / SECOND_FIX)) + ADAM_EPS
    )
    out_params[0] = old - INNER_RATE * (direction + DECAY_WEIGHT * old)
    out_first[0] = new_first
    out_second[0] = new_second


def inner_update(rows, gradient, params, first, second):
    vmem = pl.BlockSpec(memory_space=pltpu.VMEM)
    block = jax.ShapeDtypeStruct((1, FEAT, COLS), jnp.float32)
    return pl.pallas_call(
        update_kernel,
        in_specs=[vmem] * 5,
        out_specs=[vmem] * 3,
        out_shape=[block, block, block],
        cost_estimate=pl.CostEstimate(
            flops=16 * FEAT * COLS, bytes_accessed=2**20, transcendentals=2 * FEAT * COLS
        ),
        name="inner_update",
    )(rows, gradient, params, first, second)


def swap_x(block, k):
    return lax.ppermute(block, ("xp", "xb"), [(i, i ^ k) for i in range(XL)])


def add_replica(value, step):
    return value + lax.ppermute(value, "z", [(i, i ^ step) for i in range(8)])


def worker_gradient(hidden_in, norm_gain, key_cotangent, local_layer):
    place = jnp.stack([lax.axis_index(("xp", "xb")), lax.axis_index("c")]).astype(jnp.int32)
    in_hbm = functools.partial(pltpu.with_memory_space_constraint, memory_space=pltpu.HBM)
    hidden_in, norm_gain, key_cotangent = map(in_hbm, (hidden_in, norm_gain, key_cotangent))
    other_layer = lax.ppermute(local_layer, "z", [(i, i ^ 2) for i in range(8)])
    keep, send = split_norm(place, hidden_in, norm_gain, key_cotangent)
    recv = lax.ppermute(send, "c", [(0, 1), (1, 0)])
    x_wide, y_wide = chip_partial(place, in_hbm(keep), recv, key_cotangent)

    y_half = y_wide.astype(jnp.float16).reshape(YN * XL // 2, 2, HC, FEAT)
    y_half, other_layer = lax.optimization_barrier((y_half, other_layer))
    y_parts = lax.all_to_all(y_half, ("xb", "y"), 0, 0, tiled=True)
    local_layer = local_layer + other_layer
    x_sum = x_wide[0]
    for k in range(1, XL):
        x_sum = x_sum + swap_x(x_wide[k].astype(jnp.float16), k).astype(jnp.float32)
    summed = add_replica(local_layer, 4)
    x_sum = (x_sum * (X_SCALE / CHIP_SCALE)).astype(jnp.float16)
    x_sum, y_parts, summed = lax.optimization_barrier((x_sum, y_parts, summed))
    y_sum = jnp.sum(y_parts.astype(jnp.float32) * (Y_SCALE / CHIP_SCALE), axis=0)

    top = lax.all_to_all(x_sum, "y", 0, 0, tiled=True)
    bottom = y_sum[0] + swap_x(y_sum[1].astype(jnp.float16), 2).astype(jnp.float32)
    top = jnp.sum(top.astype(jnp.float32), axis=0)
    return top, bottom, add_replica(summed, 1)


def on_device(
    hidden_in,
    norm_gain,
    key_cotangent,
    inner_params,
    inner_first,
    inner_second,
    frag_local,
    frag_global,
    outer_momentum,
    frag_index,
):
    layer_index = frag_index[0]
    local_layer = lax.dynamic_index_in_dim(frag_local[0], layer_index, 0, keepdims=False)
    top, bottom, summed = worker_gradient(hidden_in, norm_gain, key_cotangent, local_layer)
    gradient, rows = turn_and_square(top, bottom)
    rows = lax.all_to_all(rows, ("xp", "xb", "y", "c", "xh"), 0, 0, tiled=True)
    new_params, new_first, new_second = inner_update(
        rows, gradient, inner_params, inner_first, inner_second
    )

    global_layer = lax.dynamic_index_in_dim(frag_global, layer_index, 0, keepdims=False)
    moment_layer = lax.dynamic_index_in_dim(outer_momentum, layer_index, 0, keepdims=False)
    workers = lax.axis_size("z")
    new_fragment, new_momentum = outer_update(summed, global_layer, moment_layer, workers)
    return (new_params, new_first, new_second, new_fragment, new_momentum)


def solution(mesh):
    workers = mesh.shape["replica"]
    devices = mesh.devices.reshape(workers, XL // 2, 2, YN, CORES, XH)
    split = Mesh(devices, ("z", "xp", "xb", "y", "c", "xh"))
    fsdp = ("xp", "xb", "y", "c")
    return jax.shard_map(
        on_device,
        mesh=split,
        in_specs=(
            P(("z",) + fsdp, None),
            P(),
            P(("z",) + fsdp, "xh"),
            P("z", fsdp, "xh"),
            P("z", fsdp, "xh"),
            P("z", fsdp, "xh"),
            P("z", None, fsdp, "xh"),
            P(None, fsdp, "xh"),
            P(None, fsdp, "xh"),
            P(),
        ),
        out_specs=(
            P("z", fsdp, "xh"),
            P("z", fsdp, "xh"),
            P("z", fsdp, "xh"),
            P(fsdp, "xh"),
            P(fsdp, "xh"),
        ),
        check_vma=False,
    )
```

```python
import functools

import jax
import jax.numpy as jnp
from jax import lax
from jax.experimental import pallas as pl
from jax.experimental.pallas import tpu as pltpu
from jax.sharding import Mesh, PartitionSpec as P

NORM_EPS = 1e-05
CLIP_RMS = 8.0
FIRST_BETA = 0.9
SECOND_BETA = 0.95
FIRST_FIX = 1.0 - 0.9**10
SECOND_FIX = 1.0 - 0.95**10
ADAM_EPS = 1e-08
INNER_RATE = 0.01
DECAY_WEIGHT = 0.1
OUTER_RATE = 0.7
OUTER_BETA = 0.9

XL, YN, CORES, XH = 4, 8, 2, 2
PEERS = XL * YN * CORES * XH
TOK, COLS, FEAT = 128, 256, 128
HALF = XL * YN * FEAT
WIDE = HALF * CORES
HC = COLS // 2
NORM_ROWS = 64
CHIP_SCALE = 2.0**-8
X_SCALE = 2.0**-10
Y_SCALE = 2.0**-12
VMEM_BYTES = 24 * 2**20


def outer_update(summed, global_layer, moment_layer, workers):
    pseudo = global_layer - summed / workers
    new_momentum = OUTER_BETA * moment_layer + pseudo
    new_fragment = global_layer - OUTER_RATE * (pseudo + OUTER_BETA * new_momentum)
    return (new_fragment, new_momentum)


def norm_kernel(place, hidden, gain, cot, keep, send):
    send[:, HALF:] = cot[...]
    widened = hidden[...].astype(jnp.float32)
    mean_square = jnp.sum(widened * widened, axis=1, keepdims=True) * (1.0 / WIDE)
    inverse = lax.rsqrt(mean_square + NORM_EPS)
    first_core = place[1] == 0
    for block in range(XL * YN):
        pair = []
        for core in range(CORES):
            at = (block * CORES + core) * FEAT
            part = hidden[:, at : at + FEAT].astype(jnp.float32)
            scale = gain[at : at + FEAT].astype(jnp.float32)[None, :]
            pair.append((part * inverse * scale).astype(jnp.bfloat16))
        out = slice(block * FEAT, (block + 1) * FEAT)
        keep[:, out] = jnp.where(first_core, pair[0], pair[1])
        send[:, out] = jnp.where(first_core, pair[1], pair[0])


def split_norm(place, hidden_in, norm_gain, cot):
    def rows(width):
        return pl.BlockSpec((NORM_ROWS, width), lambda i, place: (i, 0))

    return pl.pallas_call(
        norm_kernel,
        grid_spec=pltpu.PrefetchScalarGridSpec(
            num_scalar_prefetch=1,
            grid=(TOK // NORM_ROWS,),
            in_specs=[
                rows(WIDE),
                pl.BlockSpec((WIDE,), lambda i, place: (0,)),
                rows(COLS),
            ],
            out_specs=[rows(HALF), rows(HALF + COLS)],
        ),
        out_shape=[
            pltpu.HBM((TOK, HALF), jnp.bfloat16),
            pltpu.HBM((TOK, HALF + COLS), jnp.bfloat16),
        ],
        cost_estimate=pl.CostEstimate(
            flops=8 * TOK * WIDE, bytes_accessed=4 * TOK * WIDE, transcendentals=TOK
        ),
        compiler_params=pltpu.CompilerParams(vmem_limit_bytes=VMEM_BYTES),
        name="split_norm",
    )(place, hidden_in, norm_gain, cot)


def partial_kernel(place, keep, recv, cot, other_cot, x_out, y_out, turned):
    @pl.when(pl.program_id(0) == 0)
    def _():
        turned[:, :TOK] = cot[...].T
        turned[:, TOK:] = other_cot[...].T

    contract = (((1,), (0,)), ((), ()))
    width = YN * FEAT
    for near in range(2):
        dest = (place[0] ^ near) & 1
        chunk = pl.ds(pl.multiple_of(dest * width, width), width)
        product = lax.dot_general(
            turned[:, :TOK], keep[:, chunk], contract, preferred_element_type=jnp.float32
        ) + lax.dot_general(
            turned[:, TOK:], recv[:, chunk], contract, preferred_element_type=jnp.float32
        )
        product = product * CHIP_SCALE
        for row in range(YN):
            block = product[:, row * FEAT : (row + 1) * FEAT]
            x_out[near, row] = block[:HC]
            y_out[dest, row, 0] = block[HC:]


def chip_partial(place, keep, recv, cot):
    chunk = pl.BlockSpec((TOK, 2 * YN * FEAT), lambda far, place: (0, (place[0] // 2) ^ far))
    mine = pl.BlockSpec((TOK, COLS), lambda far, place: (0, 0))
    other = pl.BlockSpec((TOK, COLS), lambda far, place: (0, HALF // COLS))
    return pl.pallas_call(
        partial_kernel,
        grid_spec=pltpu.PrefetchScalarGridSpec(
            num_scalar_prefetch=1,
            grid=(XL // 2,),
            in_specs=[chunk, chunk, mine, other],
            out_specs=[
                pl.BlockSpec((2, YN, HC, FEAT), lambda far, place: (far, 0, 0, 0)),
                pl.BlockSpec((2, YN, 1, HC, FEAT), lambda far, place: (0, 0, far, 0, 0)),
            ],
            scratch_shapes=[pltpu.VMEM((COLS, CORES * TOK), jnp.bfloat16)],
        ),
        out_shape=[
            jax.ShapeDtypeStruct((XL, YN, HC, FEAT), jnp.float32),
            jax.ShapeDtypeStruct((XL // 2, YN, 2, HC, FEAT), jnp.float32),
        ],
        cost_estimate=pl.CostEstimate(
            flops=4 * TOK * HALF * COLS, bytes_accessed=6 * 2**20, transcendentals=0
        ),
        compiler_params=pltpu.CompilerParams(vmem_limit_bytes=VMEM_BYTES),
        name="chip_partial",
    )(place, keep, recv, cot, recv)


def square_kernel(top, bottom, gradient, rows):
    upper, lower = top[...] * (1.0 / X_SCALE), bottom[...] * (1.0 / Y_SCALE)
    gradient[:, :HC] = upper.T
    gradient[:, HC:] = lower.T
    total = jnp.sum(upper * upper + lower * lower)
    rows[...] = jnp.full(rows.shape, total, jnp.float32)


def turn_and_square(top, bottom):
    return pl.pallas_call(
        square_kernel,
        in_specs=[pl.BlockSpec(memory_space=pltpu.VMEM)] * 2,
        out_specs=[pl.BlockSpec(memory_space=pltpu.VMEM)] * 2,
        out_shape=[
            jax.ShapeDtypeStruct((FEAT, COLS), jnp.float32),
            jax.ShapeDtypeStruct((PEERS, 1, 128), jnp.float32),
        ],
        cost_estimate=pl.CostEstimate(
            flops=4 * FEAT * COLS, bytes_accessed=2**18, transcendentals=0
        ),
        name="turn_and_square",
    )(top, bottom)


def update_kernel(rows, gradient, params, first, second, out_params, out_first, out_second):
    total_square = jnp.sum(jnp.sum(rows[...], axis=0), axis=1, keepdims=True) * (1.0 / 128)
    entries = FEAT * COLS * PEERS
    factor = jnp.minimum(1.0, CLIP_RMS * lax.rsqrt(total_square * (1.0 / entries) + 1e-06))
    clipped = factor * gradient[...]
    old = params[0]
    new_first = FIRST_BETA * first[0] + (1.0 - FIRST_BETA) * clipped
    new_second = SECOND_BETA * second[0] + (1.0 - SECOND_BETA) * clipped * clipped
    direction = new_first * (1.0 / FIRST_FIX) / (
        jnp.sqrt(new_second * (1.0 / SECOND_FIX)) + ADAM_EPS
    )
    out_params[0] = old - INNER_RATE * (direction + DECAY_WEIGHT * old)
    out_first[0] = new_first
    out_second[0] = new_second


def inner_update(rows, gradient, params, first, second):
    vmem = pl.BlockSpec(memory_space=pltpu.VMEM)
    block = jax.ShapeDtypeStruct((1, FEAT, COLS), jnp.float32)
    return pl.pallas_call(
        update_kernel,
        in_specs=[vmem] * 5,
        out_specs=[vmem] * 3,
        out_shape=[block, block, block],
        cost_estimate=pl.CostEstimate(
            flops=16 * FEAT * COLS, bytes_accessed=2**20, transcendentals=2 * FEAT * COLS
        ),
        name="inner_update",
    )(rows, gradient, params, first, second)


def swap_x(block, k):
    return lax.ppermute(block, ("xp", "xb"), [(i, i ^ k) for i in range(XL)])


def add_replica(value, step):
    return value + lax.ppermute(value, "z", [(i, i ^ step) for i in range(8)])


def worker_gradient(hidden_in, norm_gain, key_cotangent, local_layer):
    place = jnp.stack([lax.axis_index(("xp", "xb")), lax.axis_index("c")]).astype(jnp.int32)
    in_hbm = functools.partial(pltpu.with_memory_space_constraint, memory_space=pltpu.HBM)
    hidden_in, norm_gain, key_cotangent = map(in_hbm, (hidden_in, norm_gain, key_cotangent))
    other_layer = lax.ppermute(local_layer, "z", [(i, i ^ 1) for i in range(8)])
    keep, send = split_norm(place, hidden_in, norm_gain, key_cotangent)
    recv = lax.ppermute(send, "c", [(0, 1), (1, 0)])
    x_wide, y_wide = chip_partial(place, in_hbm(keep), recv, key_cotangent)

    y_half = y_wide.astype(jnp.float16).reshape(YN * XL // 2, 2, HC, FEAT)
    y_half, other_layer = lax.optimization_barrier((y_half, other_layer))
    y_parts = lax.all_to_all(y_half, ("xb", "y"), 0, 0, tiled=True)
    local_layer = local_layer + other_layer
    x_sum = x_wide[0]
    for k in reversed(range(1, XL)):
        x_sum = x_sum + swap_x(x_wide[k].astype(jnp.float16), k).astype(jnp.float32)
    summed = add_replica(local_layer, 4)
    x_sum = (x_sum * (X_SCALE / CHIP_SCALE)).astype(jnp.float16)
    x_sum, y_parts, summed = lax.optimization_barrier((x_sum, y_parts, summed))
    y_sum = jnp.sum(y_parts.astype(jnp.float32) * (Y_SCALE / CHIP_SCALE), axis=0)

    top = lax.all_to_all(x_sum, "y", 0, 0, tiled=True)
    bottom = y_sum[0] + swap_x(y_sum[1].astype(jnp.float16), 2).astype(jnp.float32)
    top = jnp.sum(top.astype(jnp.float32), axis=0)
    return top, bottom, add_replica(summed, 2)


def on_device(
    hidden_in,
    norm_gain,
    key_cotangent,
    inner_params,
    inner_first,
    inner_second,
    frag_local,
    frag_global,
    outer_momentum,
    frag_index,
):
    layer_index = frag_index[0]
    local_layer = lax.dynamic_index_in_dim(frag_local[0], layer_index, 0, keepdims=False)
    top, bottom, summed = worker_gradient(hidden_in, norm_gain, key_cotangent, local_layer)
    gradient, rows = turn_and_square(top, bottom)
    rows = lax.all_to_all(rows, ("xp", "xb", "y", "c", "xh"), 0, 0, tiled=True)
    new_params, new_first, new_second = inner_update(
        rows, gradient, inner_params, inner_first, inner_second
    )

    global_layer = lax.dynamic_index_in_dim(frag_global, layer_index, 0, keepdims=False)
    moment_layer = lax.dynamic_index_in_dim(outer_momentum, layer_index, 0, keepdims=False)
    workers = lax.axis_size("z")
    new_fragment, new_momentum = outer_update(summed, global_layer, moment_layer, workers)
    return (new_params, new_first, new_second, new_fragment, new_momentum)


def solution(mesh):
    workers = mesh.shape["replica"]
    devices = mesh.devices.reshape(workers, XL // 2, 2, YN, CORES, XH)
    split = Mesh(devices, ("z", "xp", "xb", "y", "c", "xh"))
    fsdp = ("xp", "xb", "y", "c")
    return jax.shard_map(
        on_device,
        mesh=split,
        in_specs=(
            P(("z",) + fsdp, None),
            P(),
            P(("z",) + fsdp, "xh"),
            P("z", fsdp, "xh"),
            P("z", fsdp, "xh"),
            P("z", fsdp, "xh"),
            P("z", None, fsdp, "xh"),
            P(None, fsdp, "xh"),
            P(None, fsdp, "xh"),
            P(),
        ),
        out_specs=(
            P("z", fsdp, "xh"),
            P("z", fsdp, "xh"),
            P("z", fsdp, "xh"),
            P(fsdp, "xh"),
            P(fsdp, "xh"),
        ),
        check_vma=False,
    )
```

```python
import functools

import jax
import jax.numpy as jnp
from jax import lax
from jax.experimental import pallas as pl
from jax.experimental.pallas import tpu as pltpu
from jax.sharding import Mesh, PartitionSpec as P

NORM_EPS = 1e-05
CLIP_RMS = 8.0
FIRST_BETA = 0.9
SECOND_BETA = 0.95
FIRST_FIX = 1.0 - 0.9**10
SECOND_FIX = 1.0 - 0.95**10
ADAM_EPS = 1e-08
INNER_RATE = 0.01
DECAY_WEIGHT = 0.1
OUTER_RATE = 0.7
OUTER_BETA = 0.9

XL, YN, CORES, XH = 4, 8, 2, 2
PEERS = XL * YN * CORES * XH
TOK, COLS, FEAT = 128, 256, 128
HALF = XL * YN * FEAT
WIDE = HALF * CORES
XC, YC = 96, COLS - 96
NORM_ROWS = 64
CHIP_SCALE = 2.0**-8
X_SCALE = 2.0**-10
Y_SCALE = 2.0**-12
VMEM_BYTES = 24 * 2**20


def outer_update(summed, global_layer, moment_layer, workers):
    pseudo = global_layer - summed / workers
    new_momentum = OUTER_BETA * moment_layer + pseudo
    new_fragment = global_layer - OUTER_RATE * (pseudo + OUTER_BETA * new_momentum)
    return (new_fragment, new_momentum)


def norm_kernel(place, hidden, gain, cot, keep, send):
    send[:, HALF:] = cot[...]
    widened = hidden[...].astype(jnp.float32)
    mean_square = jnp.sum(widened * widened, axis=1, keepdims=True) * (1.0 / WIDE)
    inverse = lax.rsqrt(mean_square + NORM_EPS)
    first_core = place[1] == 0
    for block in range(XL * YN):
        pair = []
        for core in range(CORES):
            at = (block * CORES + core) * FEAT
            part = hidden[:, at : at + FEAT].astype(jnp.float32)
            scale = gain[at : at + FEAT].astype(jnp.float32)[None, :]
            pair.append((part * inverse * scale).astype(jnp.bfloat16))
        out = slice(block * FEAT, (block + 1) * FEAT)
        keep[:, out] = jnp.where(first_core, pair[0], pair[1])
        send[:, out] = jnp.where(first_core, pair[1], pair[0])


def split_norm(place, hidden_in, norm_gain, cot):
    def rows(width):
        return pl.BlockSpec((NORM_ROWS, width), lambda i, place: (i, 0))

    return pl.pallas_call(
        norm_kernel,
        grid_spec=pltpu.PrefetchScalarGridSpec(
            num_scalar_prefetch=1,
            grid=(TOK // NORM_ROWS,),
            in_specs=[
                rows(WIDE),
                pl.BlockSpec((WIDE,), lambda i, place: (0,)),
                rows(COLS),
            ],
            out_specs=[rows(HALF), rows(HALF + COLS)],
        ),
        out_shape=[
            pltpu.HBM((TOK, HALF), jnp.bfloat16),
            pltpu.HBM((TOK, HALF + COLS), jnp.bfloat16),
        ],
        cost_estimate=pl.CostEstimate(
            flops=8 * TOK * WIDE, bytes_accessed=4 * TOK * WIDE, transcendentals=TOK
        ),
        compiler_params=pltpu.CompilerParams(vmem_limit_bytes=VMEM_BYTES),
        name="split_norm",
    )(place, hidden_in, norm_gain, cot)


def partial_kernel(place, keep, recv, cot, other_cot, x_out, y_out, turned):
    @pl.when(pl.program_id(0) == 0)
    def _():
        turned[:, :TOK] = cot[...].T
        turned[:, TOK:] = other_cot[...].T

    contract = (((1,), (0,)), ((), ()))
    width = YN * FEAT
    for near in range(2):
        dest = (place[0] ^ near) & 1
        chunk = pl.ds(pl.multiple_of(dest * width, width), width)
        product = lax.dot_general(
            turned[:, :TOK], keep[:, chunk], contract, preferred_element_type=jnp.float32
        ) + lax.dot_general(
            turned[:, TOK:], recv[:, chunk], contract, preferred_element_type=jnp.float32
        )
        product = product * CHIP_SCALE
        for row in range(YN):
            block = product[:, row * FEAT : (row + 1) * FEAT]
            x_out[near, row] = block[:XC]
            y_out[dest, row, 0] = block[XC:]


def chip_partial(place, keep, recv, cot):
    chunk = pl.BlockSpec((TOK, 2 * YN * FEAT), lambda far, place: (0, (place[0] // 2) ^ far))
    mine = pl.BlockSpec((TOK, COLS), lambda far, place: (0, 0))
    other = pl.BlockSpec((TOK, COLS), lambda far, place: (0, HALF // COLS))
    return pl.pallas_call(
        partial_kernel,
        grid_spec=pltpu.PrefetchScalarGridSpec(
            num_scalar_prefetch=1,
            grid=(XL // 2,),
            in_specs=[chunk, chunk, mine, other],
            out_specs=[
                pl.BlockSpec((2, YN, XC, FEAT), lambda far, place: (far, 0, 0, 0)),
                pl.BlockSpec((2, YN, 1, YC, FEAT), lambda far, place: (0, 0, far, 0, 0)),
            ],
            scratch_shapes=[pltpu.VMEM((COLS, CORES * TOK), jnp.bfloat16)],
        ),
        out_shape=[
            jax.ShapeDtypeStruct((XL, YN, XC, FEAT), jnp.float32),
            jax.ShapeDtypeStruct((XL // 2, YN, 2, YC, FEAT), jnp.float32),
        ],
        cost_estimate=pl.CostEstimate(
            flops=4 * TOK * HALF * COLS, bytes_accessed=6 * 2**20, transcendentals=0
        ),
        compiler_params=pltpu.CompilerParams(vmem_limit_bytes=VMEM_BYTES),
        name="chip_partial",
    )(place, keep, recv, cot, recv)


def square_kernel(top, bottom, gradient, rows):
    upper, lower = top[...] * (1.0 / X_SCALE), bottom[...] * (1.0 / Y_SCALE)
    both = jnp.concatenate([upper, lower], axis=0)
    gradient[...] = both.T
    total = jnp.sum(both * both)
    rows[...] = jnp.full(rows.shape, total, jnp.float32)


def turn_and_square(top, bottom):
    return pl.pallas_call(
        square_kernel,
        in_specs=[pl.BlockSpec(memory_space=pltpu.VMEM)] * 2,
        out_specs=[pl.BlockSpec(memory_space=pltpu.VMEM)] * 2,
        out_shape=[
            jax.ShapeDtypeStruct((FEAT, COLS), jnp.float32),
            jax.ShapeDtypeStruct((PEERS, 1, 128), jnp.float32),
        ],
        cost_estimate=pl.CostEstimate(
            flops=4 * FEAT * COLS, bytes_accessed=2**18, transcendentals=0
        ),
        name="turn_and_square",
    )(top, bottom)


def update_kernel(rows, gradient, params, first, second, out_params, out_first, out_second):
    total_square = jnp.sum(jnp.sum(rows[...], axis=0), axis=1, keepdims=True) * (1.0 / 128)
    entries = FEAT * COLS * PEERS
    factor = jnp.minimum(1.0, CLIP_RMS * lax.rsqrt(total_square * (1.0 / entries) + 1e-06))
    clipped = factor * gradient[...]
    old = params[0]
    new_first = FIRST_BETA * first[0] + (1.0 - FIRST_BETA) * clipped
    new_second = SECOND_BETA * second[0] + (1.0 - SECOND_BETA) * clipped * clipped
    direction = new_first * (1.0 / FIRST_FIX) / (
        jnp.sqrt(new_second * (1.0 / SECOND_FIX)) + ADAM_EPS
    )
    out_params[0] = old - INNER_RATE * (direction + DECAY_WEIGHT * old)
    out_first[0] = new_first
    out_second[0] = new_second


def inner_update(rows, gradient, params, first, second):
    vmem = pl.BlockSpec(memory_space=pltpu.VMEM)
    block = jax.ShapeDtypeStruct((1, FEAT, COLS), jnp.float32)
    return pl.pallas_call(
        update_kernel,
        in_specs=[vmem] * 5,
        out_specs=[vmem] * 3,
        out_shape=[block, block, block],
        cost_estimate=pl.CostEstimate(
            flops=16 * FEAT * COLS, bytes_accessed=2**20, transcendentals=2 * FEAT * COLS
        ),
        name="inner_update",
    )(rows, gradient, params, first, second)


def swap_x(block, k):
    return lax.ppermute(block, ("xp", "xb"), [(i, i ^ k) for i in range(XL)])


def add_replica(value, step):
    return value + lax.ppermute(value, "z", [(i, i ^ step) for i in range(8)])


def worker_gradient(hidden_in, norm_gain, key_cotangent, local_layer):
    place = jnp.stack([lax.axis_index(("xp", "xb")), lax.axis_index("c")]).astype(jnp.int32)
    in_hbm = functools.partial(pltpu.with_memory_space_constraint, memory_space=pltpu.HBM)
    hidden_in, norm_gain, key_cotangent = map(in_hbm, (hidden_in, norm_gain, key_cotangent))
    other_layer = lax.ppermute(local_layer, "z", [(i, i ^ 1) for i in range(8)])
    keep, send = split_norm(place, hidden_in, norm_gain, key_cotangent)
    recv = lax.ppermute(send, "c", [(0, 1), (1, 0)])
    x_wide, y_wide = chip_partial(place, in_hbm(keep), recv, key_cotangent)

    y_half = y_wide.astype(jnp.float16).reshape(YN * XL // 2, 2, YC, FEAT)
    y_half, other_layer = lax.optimization_barrier((y_half, other_layer))
    y_parts = lax.all_to_all(y_half, ("xb", "y"), 0, 0, tiled=True)
    local_layer = local_layer + other_layer
    x_sum = x_wide[0]
    for k in reversed(range(1, XL)):
        x_sum = x_sum + swap_x(x_wide[k].astype(jnp.float16), k).astype(jnp.float32)
    summed = add_replica(local_layer, 4)
    x_sum = (x_sum * (X_SCALE / CHIP_SCALE)).astype(jnp.float16)
    x_sum, y_parts, summed = lax.optimization_barrier((x_sum, y_parts, summed))
    y_sum = jnp.sum(y_parts.astype(jnp.float32) * (Y_SCALE / CHIP_SCALE), axis=0)

    top = lax.all_to_all(x_sum, "y", 0, 0, tiled=True)
    bottom = y_sum[0] + swap_x(y_sum[1].astype(jnp.float16), 2).astype(jnp.float32)
    top = jnp.sum(top.astype(jnp.float32), axis=0)
    return top, bottom, add_replica(summed, 2)


def on_device(
    hidden_in,
    norm_gain,
    key_cotangent,
    inner_params,
    inner_first,
    inner_second,
    frag_local,
    frag_global,
    outer_momentum,
    frag_index,
):
    layer_index = frag_index[0]
    local_layer = lax.dynamic_index_in_dim(frag_local[0], layer_index, 0, keepdims=False)
    top, bottom, summed = worker_gradient(hidden_in, norm_gain, key_cotangent, local_layer)
    gradient, rows = turn_and_square(top, bottom)
    rows = lax.all_to_all(rows, ("xp", "xb", "y", "c", "xh"), 0, 0, tiled=True)
    new_params, new_first, new_second = inner_update(
        rows, gradient, inner_params, inner_first, inner_second
    )

    global_layer = lax.dynamic_index_in_dim(frag_global, layer_index, 0, keepdims=False)
    moment_layer = lax.dynamic_index_in_dim(outer_momentum, layer_index, 0, keepdims=False)
    workers = lax.axis_size("z")
    new_fragment, new_momentum = outer_update(summed, global_layer, moment_layer, workers)
    return (new_params, new_first, new_second, new_fragment, new_momentum)


def solution(mesh):
    workers = mesh.shape["replica"]
    devices = mesh.devices.reshape(workers, XL // 2, 2, YN, CORES, XH)
    split = Mesh(devices, ("z", "xp", "xb", "y", "c", "xh"))
    fsdp = ("xp", "xb", "y", "c")
    return jax.shard_map(
        on_device,
        mesh=split,
        in_specs=(
            P(("z",) + fsdp, None),
            P(),
            P(("z",) + fsdp, "xh"),
            P("z", fsdp, "xh"),
            P("z", fsdp, "xh"),
            P("z", fsdp, "xh"),
            P("z", None, fsdp, "xh"),
            P(None, fsdp, "xh"),
            P(None, fsdp, "xh"),
            P(),
        ),
        out_specs=(
            P("z", fsdp, "xh"),
            P("z", fsdp, "xh"),
            P("z", fsdp, "xh"),
            P(fsdp, "xh"),
            P(fsdp, "xh"),
        ),
        check_vma=False,
    )
```
